32 devices in a mesh: ref: 8 (over z, x), voc: 4 (over y, core).
Axes of the slice: x: 2, y: 2, z: 4, core: 2. Of those that a mesh axis runs over, the one named last changes fastest.
Arguments:
- private_logits: bfloat16 [96, 4, 128256], P('ref', None, 'voc'), may hold values from -16 to 16
- public_logits: bfloat16 [4, 4, 128256], P(None, None, ('voc', 'ref')), may hold values from -250 to 250
- noise: bfloat16 [4, 4, 128256], P(None, None, ('voc', 'ref')), may hold values from -6 to 6
- owner: int32 [96], P('ref'), may hold values from 0 to 3, as said below
- counts: int32 [4], replicated, may hold values from 1 to 24, as said below
- tokens: int32 [4, 4], replicated, may hold values from 0 to 128255
Outputs:
- logprobs: float32 [4, 4, 128256], P(None, None, ('voc', 'ref'))
- target: float32 [4, 4], replicated
The draws below stay inside these ranges and needn't reach their ends.
Inputs may be any that keep to these rules, and one draw needn't show every extreme that they name: `owner`: each of the 4 texts owns exactly 24 rows. `counts`: the count of a text is at least half of the rows that it owns, rounded up, and at most all of them; some text keeps all of its rows.
All inputs are finite; a program needn't handle non-finite values.
Results may differ from the reference program's by a relative error of at most 0.0003.
Values may be sent and summed in bfloat16 or wider, within the bound.
A program may use at most 128 MiB of HBM per device.

```python
import jax
import jax.numpy as jnp
from jax import lax

V = 128256
TEXTS = 4
POS = 4
REF_DEV = 12
REFS = 96
N_REF = 8


def draw_public_logits(key, part):
    values = 3.0 * jax.random.normal(jax.random.fold_in(key, 21), (TEXTS, POS, V), jnp.float32)
    values = jnp.clip(values, -18.0, 18.0)
    return values.astype(jnp.bfloat16)


def split_rows(key):
    row_index = jnp.arange(REFS, dtype=jnp.int32)
    owner_rows = jax.random.permutation(jax.random.fold_in(key, 31), (row_index % TEXTS).astype(jnp.int32)).astype(jnp.int32)
    owned = jnp.full((TEXTS,), REFS // TEXTS, dtype=jnp.int32)
    removed = jax.random.randint(jax.random.fold_in(key, 32), (TEXTS,), 0, owned // 2 + 1, dtype=jnp.int32)
    keeper = jax.random.randint(jax.random.fold_in(key, 33), (), 0, TEXTS, dtype=jnp.int32)
    removed = jnp.where(jnp.arange(TEXTS, dtype=jnp.int32) == keeper, 0, removed).astype(jnp.int32)
    return (owner_rows, (owned - removed).astype(jnp.int32))


def draw_owner(key, part):
    return split_rows(key)[0]


def draw_counts(key, part):
    return split_rows(key)[1]


def plant(values, key, smallest, largest):
    index_at = [jax.random.randint(jax.random.fold_in(key, axis), (), 0, length) for axis, length in enumerate(values.shape)]
    main_axis = values.shape.index(max(values.shape))
    beside = index_at[:main_axis] + [(index_at[main_axis] + 1) % values.shape[main_axis]] + index_at[main_axis + 1:]
    return values.at[tuple(index_at)].set(smallest).at[tuple(beside)].set(largest)


def shard_levels(own_key, shape, cuts, low, high):
    level = 1.0
    for axis_at, shards_of in cuts:
        steps = jax.random.uniform(jax.random.fold_in(jax.random.fold_in(own_key, 6), axis_at), (shards_of,), jnp.float32, low / len(cuts), high / len(cuts))
        level = level * jnp.repeat(jnp.exp(steps), shape[axis_at] // shards_of).reshape((-1,) + (1,) * (len(shape) - 1 - axis_at))
    return level


def bell_draw(stream_key, dims, width, limit, cuts=(), held_as=jnp.bfloat16):
    entries = width * jax.random.normal(stream_key, dims, jnp.float32)
    if cuts:
        entries = entries * shard_levels(stream_key, dims, cuts, -0.22, 0.18)
    return jnp.clip(entries, -limit, limit).astype(held_as)


def setup_inputs(seed: int = 0) -> dict:
    key_list = jax.random.split(jax.random.key(seed), 7)
    return {
        "private_logits": bell_draw(key_list[0], (REFS, POS, V), 3.0, 16.0, ((0, 8), (2, 4))),
        "public_logits": draw_public_logits(jax.random.fold_in(key_list[6], 71), 0),
        "noise": bell_draw(key_list[2], (TEXTS, POS, V), 1.0, 6.0, ((2, 32),)),
        "owner": draw_owner(jax.random.fold_in(key_list[6], 71), 0),
        "counts": draw_counts(jax.random.fold_in(key_list[6], 71), 0),
        "tokens": plant(jax.random.randint(key_list[5], (TEXTS, POS), 0, V), jax.random.fold_in(key_list[5], 1), 0, V - 1).astype(jnp.int32),
    }


clip_bound = 2.0

def reference(private_logits, public_logits, noise, owner, counts, tokens):
    text_count = counts.shape[0]
    labels = jnp.arange(text_count, dtype=jnp.int32)
    chosen = (owner[:, None] == labels[None, :]).astype(jnp.int32)
    before = (jnp.cumsum(chosen, 0) - chosen).astype(jnp.int32)
    row_rank = lax.optimization_barrier(jnp.sum(before * chosen, 1)).astype(jnp.int32)
    row_limit = lax.optimization_barrier(jnp.sum(chosen * counts[None, :], 1)).astype(jnp.int32)
    select = chosen.astype(jnp.float32)
    weight = select * (row_rank < row_limit).astype(jnp.float32)[:, None]
    public_wide = public_logits.astype(jnp.float32)

    def accumulate(summed, pieces):
        private_piece, select_piece, weight_piece = pieces
        matched = jnp.einsum('rt,tpv->rpv', select_piece, public_wide, precision=lax.Precision.HIGHEST)
        clipped = jnp.clip(private_piece.astype(jnp.float32) - matched, -clip_bound, clip_bound)
        return (summed + jnp.einsum('rt,rpv->tpv', weight_piece, clipped, precision=lax.Precision.HIGHEST), None)
    grouped = (private_logits.reshape(N_REF, REF_DEV, POS, V), select.reshape(N_REF, REF_DEV, text_count), weight.reshape(N_REF, REF_DEV, text_count))
    summed, unused = lax.scan(accumulate, jnp.zeros((text_count, POS, V), jnp.float32), grouped)
    text_scale = 1.0 / (clip_bound * jnp.sqrt(counts.astype(jnp.float32)))
    combined = public_wide + summed * text_scale[:, None, None] + noise.astype(jnp.float32)
    row_peak = lax.optimization_barrier(jnp.max(combined, axis=2))
    lse = row_peak + jnp.log(lax.optimization_barrier(jnp.sum(jnp.exp(combined - row_peak[:, :, None]), axis=2)))
    logprobs = combined - lse[:, :, None]
    target = jnp.take_along_axis(logprobs, tokens[:, :, None], axis=2)[:, :, 0]
    return (logprobs, target)
```

```python
import functools

import jax
import jax.numpy as jnp
from jax import lax
from jax.experimental import pallas as pl
from jax.experimental.pallas import tpu as pltpu
from jax.sharding import PartitionSpec as P

clip_bound = 2.0
LANES = 128
MESH = pl.DeviceIdType.MESH


def fixed_point(rows):
    scale = 1
    while scale * 2 * clip_bound * rows <= 32000:
        scale *= 2
    return float(scale)


def kernel(
    n, nv, rows, texts, pos, width, piece, win,
    owner, counts, tokens, priv, pub, noise,
    combined_out, stats_out,
    pv, xt, pubf, pubs, here, pref, keep, snd1, rs1, snd2, rs2,
    hist, st1, st2, bnd, order, sown, start,
    priv_sem, hist_s, hist_r, ag_s, ag_f, ag_r, rs1_s, rs1_r, rs2_s, rs2_r,
    st1_s, st1_r, st2_s, st2_r,
):
    f32 = jnp.float32
    half = n // 2
    full = width // LANES
    wl = win * LANES
    me = lax.axis_index("ref")
    mv = lax.axis_index("voc")
    z = lax.div(me, 2)
    x = lax.rem(me, 2)
    partner = me + 1 - 2 * x
    scale1 = fixed_point(rows)
    scale2 = fixed_point(2 * rows)

    def first_tile(j):
        return jnp.minimum(lax.div(j * piece, LANES), full + 1 - win)

    def remote(src, dst, send, recv, peer):
        return pltpu.make_async_remote_copy(
            src_ref=src, dst_ref=dst, send_sem=send, recv_sem=recv,
            device_id=peer, device_id_type=MESH,
        )

    load = pltpu.make_async_copy(priv, pv, priv_sem)
    load.start()
    barrier = pltpu.get_barrier_semaphore()

    def greet(k, c):
        pl.semaphore_signal(barrier, inc=1, device_id={"ref": lax.rem(me + k, n)}, device_id_type=MESH)
        return c

    def greet_voc(k, c):
        pl.semaphore_signal(barrier, inc=1, device_id={"voc": lax.rem(mv + k, nv)}, device_id_type=MESH)
        return c

    lax.fori_loop(1, n, greet, 0)
    lax.fori_loop(1, nv, greet_voc, 0)

    shift = me * piece - first_tile(me) * LANES
    pubf[...] = jnp.zeros_like(pubf)
    for t in range(texts):
        pubf[t, :, :piece] = pub[t].astype(f32)
    for t in range(texts):
        pubs[me, t] = pltpu.roll(pubf[t], shift, 1).astype(jnp.bfloat16)

    own = [owner[r] for r in range(rows)]
    hits = [sum((o == t).astype(jnp.int32) for o in own) for t in range(texts)]
    begin = [jnp.int32(0)]
    for t in range(texts):
        begin.append(begin[-1] + hits[t])
    for t in range(texts + 1):
        start[t] = begin[t]
    place = []
    for r in range(rows):
        before = jnp.int32(0)
        for q in range(rows):
            if q < r:
                before = before + (own[q] <= own[r]).astype(jnp.int32)
            elif q > r:
                before = before + (own[q] < own[r]).astype(jnp.int32)
        place.append(before)
    for k in range(rows):
        at = jnp.int32(0)
        for r in range(rows):
            at = at + jnp.where(place[r] == k, r, 0)
        order[k] = at
        sown[k] = sum((begin[t] <= k).astype(jnp.int32) for t in range(1, texts))

    lane8 = lax.broadcasted_iota(jnp.int32, (8, LANES), 1)
    mine = jnp.zeros((8, LANES), jnp.int32)
    for t in range(texts):
        mine = jnp.where(lane8 == t, hits[t], mine)
    hist[me] = mine

    pl.semaphore_wait(barrier, n - 1 + nv - 1)

    def send_hist(k, c):
        remote(hist.at[me], hist.at[me], hist_s, hist_r, {"ref": lax.rem(me + k, n)}).start()
        return c

    lax.fori_loop(1, n, send_hist, 0)
    remote(pubs.at[me], pubs.at[me], ag_s.at[0], ag_r.at[me], {"ref": partner}).start()

    def send_own(k, c):
        peer = 2 * lax.rem(z + k, half) + x
        remote(pubs.at[me], pubs.at[me], ag_s.at[k], ag_r.at[me], {"ref": peer}).start()
        return c

    lax.fori_loop(1, half, send_own, 0)

    load.wait()
    for j in range(n):
        s = min(j * piece // LANES, full + 1 - win) + win - 1
        if s < full:
            xt[:, :, j * LANES:(j + 1) * LANES] = pv[:, :, s * LANES:(s + 1) * LANES]
        else:
            xt[:, :, j * LANES:(j + 1) * LANES] = jnp.zeros((rows, pos, LANES), jnp.bfloat16)
            if width > full * LANES:
                xt[:, :, j * LANES:j * LANES + width - full * LANES] = pv[:, :, full * LANES:]

    got = hist.at[pl.ds(0, n - 1)]
    pltpu.make_async_copy(got, got, hist_r).wait()
    pltpu.make_async_copy(got, got, hist_s).wait()
    lower = jnp.zeros((8, LANES), jnp.int32)
    lower = lax.fori_loop(0, n, lambda j, a: a + jnp.where(j < me, hist[j], 0), lower)
    lower = lower[:pos]
    lane4 = lax.broadcasted_iota(jnp.int32, (pos, LANES), 1)
    for k in range(rows):
        text = sown[k]
        limit = counts[text] - (k - start[text])
        ok = jnp.where((lane4 == text) & (lower < limit), clip_bound, 0.0)
        bnd[k] = jnp.broadcast_to(jnp.max(ok, axis=1, keepdims=True), (pos, LANES))

    tiles = max(c for c in range(1, 9) if (win - 1) % c == 0)

    def partial_sums(j, store):
        base = first_tile(j)
        for t in range(texts):
            here[t] = pubs[j, t].astype(f32)

        def some(count, source, at, to):
            acc = [jnp.zeros((pos, LANES), f32)] * count
            for c in range(count):
                pref[0, :, c * LANES:(c + 1) * LANES] = acc[c]
            for k in range(rows):
                row = order[k]
                text = sown[k]
                b = bnd[k]
                for c in range(count):
                    p = source[row, :, pl.ds(pl.multiple_of(at + c * LANES, LANES), LANES)].astype(f32)
                    u = here[text, :, pl.ds(pl.multiple_of(to + c * LANES, LANES), LANES)]
                    acc[c] = acc[c] + jnp.minimum(jnp.maximum(p - u, -b), b)
                    pref[k + 1, :, c * LANES:(c + 1) * LANES] = acc[c]
            for t in range(texts):
                v = pref[start[t + 1], :, :count * LANES] - pref[start[t], :, :count * LANES]
                store(t, pl.ds(pl.multiple_of(to, LANES), count * LANES), v)

        def chunk(i, c):
            to = i * (tiles * LANES)
            some(tiles, pv, base * LANES + to, to)
            return c

        lax.fori_loop(0, (win - 1) // tiles, chunk, 0)
        some(1, xt, j * LANES, (win - 1) * LANES)

    def coded(v, scale):
        return jnp.round(v * scale).astype(jnp.int32).astype(jnp.int16)

    def decoded(q, scale):
        return q.astype(jnp.int32).astype(f32) * (1.0 / scale)

    def column(i):
        return lax.rem(z - i + half, half)

    def step(i, c):
        @pl.when(i < half)
        def _():
            zi = column(i)
            j = 2 * zi + x

            @pl.when(i > 0)
            def _():
                remote(pubs.at[j], pubs.at[j], ag_f.at[zi], ag_r.at[j], {"ref": partner}).wait_recv()
                remote(pubs.at[j], pubs.at[j], ag_f.at[zi], ag_r.at[j], {"ref": partner}).start()

            def store(t, lanes, v):
                keep[zi, t, :, lanes] = v

            partial_sums(j, store)

        @pl.when((i >= 1) & (i <= half))
        def _():
            zi = column(i - 1)
            j = 2 * zi + 1 - x
            remote(pubs.at[j], pubs.at[j], ag_f.at[zi], ag_r.at[j], {"ref": partner}).wait_recv()

            def store(t, lanes, v):
                snd1[zi, t, :, lanes] = coded(v, scale1)

            partial_sums(j, store)
            remote(snd1.at[zi], rs1.at[zi], rs1_s.at[zi], rs1_r.at[zi], {"ref": partner}).start()

        @pl.when(i >= 2)
        def _():
            zi = column(i - 2)
            remote(snd1.at[zi], rs1.at[zi], rs1_s.at[zi], rs1_r.at[zi], {"ref": partner}).wait_recv()

            @pl.when(i == 2)
            def _():
                for t in range(texts):
                    keep[zi, t] = keep[zi, t] + decoded(rs1[zi, t], scale1)

            @pl.when(i > 2)
            def _():
                for t in range(texts):
                    snd2[zi, t] = coded(keep[zi, t] + decoded(rs1[zi, t], scale1), scale2)
                remote(snd2.at[zi], rs2.at[z], rs2_s.at[zi], rs2_r.at[z], {"ref": 2 * zi + x}).start()

        return c

    lax.fori_loop(0, half + 2, step, 0)

    def gather(k, c):
        zi = lax.rem(z + k, half)
        remote(snd2.at[zi], rs2.at[zi], rs2_s.at[zi], rs2_r.at[zi], {"ref": 2 * zi + x}).wait_recv()
        for t in range(texts):
            keep[z, t] = keep[z, t] + decoded(rs2[zi, t], scale2)
        return c

    lax.fori_loop(1, half, gather, 0)

    first_column = (mv * n + me) * piece
    at_column = lax.broadcasted_iota(jnp.int32, (pos, piece), 1) + first_column
    at_pos = lax.broadcasted_iota(jnp.int32, (pos, 1), 0)
    lse_all = jnp.zeros((pos, LANES), f32)
    picked_all = jnp.zeros((pos, LANES), f32)
    for t in range(texts):
        summed = pltpu.roll(keep[z, t], lax.rem(wl - shift, wl), 1)[:, :piece]
        root = jnp.sqrt(jnp.full((pos, LANES), counts[t].astype(f32), f32))
        factor = (1.0 / (clip_bound * root))[:, :1]
        combined = pub[t].astype(f32) + summed * factor + noise[t].astype(f32)
        combined_out[t] = combined
        peak = jnp.max(combined, axis=1, keepdims=True)
        total = jnp.sum(jnp.exp(combined - peak), axis=1, keepdims=True)
        token = jnp.zeros((pos, 1), jnp.int32)
        for p in range(pos):
            token = jnp.where(at_pos == p, tokens[t, p], token)
        picked = jnp.sum(jnp.where(at_column == token, combined, 0.0), axis=1, keepdims=True)
        lse_all = jnp.where(lane4 == t, peak + jnp.log(total), lse_all)
        picked_all = jnp.where(lane4 == t, picked, picked_all)

    def exchange(slots, send, recv, index, count, axis, lse, picked):
        slots[index, :pos] = lse
        slots[index, pos:2 * pos] = picked

        def send_one(k, c):
            remote(slots.at[index], slots.at[index], send, recv, {axis: lax.rem(index + k, count)}).start()
            return c

        lax.fori_loop(1, count, send_one, 0)
        others = slots.at[pl.ds(0, count - 1)]
        pltpu.make_async_copy(others, others, recv).wait()
        pltpu.make_async_copy(others, others, send).wait()
        top = lax.fori_loop(1, count, lambda j, a: jnp.maximum(a, slots[j, :pos]), slots[0, :pos])
        zero = jnp.zeros((pos, LANES), f32)
        total, found = lax.fori_loop(
            0, count,
            lambda j, a: (a[0] + jnp.exp(slots[j, :pos] - top), a[1] + slots[j, pos:2 * pos]),
            (zero, zero),
        )
        return top + jnp.log(total), found

    lse, picked = exchange(st1, st1_s, st1_r, mv, nv, "voc", lse_all, picked_all)
    lse, picked = exchange(st2, st2_s, st2_r, me, n, "ref", lse, picked)
    stats_out[0] = lse
    stats_out[1] = picked

    def sent(i, c):
        remote(pubs.at[me], pubs.at[me], ag_s.at[i], ag_r.at[me], {"ref": partner}).wait_send()
        remote(snd1.at[i], rs1.at[i], rs1_s.at[i], rs1_r.at[i], {"ref": partner}).wait_send()

        @pl.when(i != z)
        def _():
            remote(pubs.at[me], pubs.at[me], ag_f.at[i], ag_r.at[me], {"ref": partner}).wait_send()
            remote(snd2.at[i], rs2.at[i], rs2_s.at[i], rs2_r.at[i], {"ref": partner}).wait_send()

        return c

    lax.fori_loop(0, half, sent, 0)


def body(n, nv, private_logits, public_logits, noise, owner, counts, tokens):
    rows, pos, width = private_logits.shape
    texts, _, piece = public_logits.shape
    half = n // 2
    full = width // LANES
    win = max(-(-((j * piece) % LANES + piece) // LANES) for j in range(n))
    while min(j * piece - LANES * min(j * piece // LANES, full + 1 - win) for j in range(n)) < 0:
        win += 1
    wl = win * LANES
    bf16, f32, i16 = jnp.bfloat16, jnp.float32, jnp.int16
    smem = pl.BlockSpec(memory_space=pltpu.SMEM)
    vmem = pl.BlockSpec(memory_space=pltpu.VMEM)
    dma = pltpu.SemaphoreType.DMA
    combined, stats = pl.pallas_call(
        functools.partial(kernel, n, nv, rows, texts, pos, width, piece, win),
        out_shape=(
            jax.ShapeDtypeStruct((texts, pos, piece), f32),
            jax.ShapeDtypeStruct((2, pos, LANES), f32),
        ),
        in_specs=[smem, smem, smem, pl.BlockSpec(memory_space=pl.ANY), vmem, vmem],
        out_specs=(vmem, vmem),
        scratch_shapes=[
            pltpu.VMEM((rows, pos, width), bf16),
            pltpu.VMEM((rows, pos, n * LANES), bf16),
            pltpu.VMEM((texts, pos, wl), f32),
            pltpu.VMEM((n, texts, pos, wl), bf16),
            pltpu.VMEM((texts, pos, wl), f32),
            pltpu.VMEM((rows + 1, pos, 8 * LANES), f32),
            pltpu.VMEM((half, texts, pos, wl), f32),
            pltpu.VMEM((half, texts, pos, wl), i16),
            pltpu.VMEM((half, texts, pos, wl), i16),
            pltpu.VMEM((half, texts, pos, wl), i16),
            pltpu.VMEM((half, texts, pos, wl), i16),
            pltpu.VMEM((n, 8, LANES), jnp.int32),
            pltpu.VMEM((nv, 2 * pos, LANES), f32),
            pltpu.VMEM((n, 2 * pos, LANES), f32),
            pltpu.VMEM((rows, pos, LANES), f32),
            pltpu.SMEM((rows,), jnp.int32),
            pltpu.SMEM((rows,), jnp.int32),
            pltpu.SMEM((texts + 1,), jnp.int32),
            dma, dma, dma,
            dma((half,)), dma((half,)), dma((n,)),
            dma((half,)), dma((half,)), dma((half,)), dma((half,)),
            dma, dma, dma, dma,
        ],
        compiler_params=pltpu.CompilerParams(
            collective_id=0, has_side_effects=True, vmem_limit_bytes=56 * 1024 * 1024
        ),
        cost_estimate=pl.CostEstimate(
            flops=6 * rows * pos * width, bytes_accessed=2 * rows * pos * width, transcendentals=0
        ),
        name="private_scores",
    )(owner, counts, tokens, private_logits, public_logits, noise)
    lse = stats[0, :, :texts].T
    logprobs = combined - lse[:, :, None]
    target = stats[1, :, :texts].T - lse
    return (logprobs, target)


def solution(mesh):
    return jax.shard_map(
        functools.partial(body, mesh.shape["ref"], mesh.shape["voc"]),
        mesh=mesh,
        in_specs=(
            P("ref", None, "voc"),
            P(None, None, ("voc", "ref")),
            P(None, None, ("voc", "ref")),
            P("ref"),
            P(),
            P(),
        ),
        out_specs=(P(None, None, ("voc", "ref")), P()),
        check_vma=False,
    )
```

```python
import functools

import jax
import jax.numpy as jnp
from jax import lax
from jax.experimental import pallas as pl
from jax.experimental.pallas import tpu as pltpu
from jax.sharding import PartitionSpec as P

clip_bound = 2.0
LANES = 128
MESH = pl.DeviceIdType.MESH


def fixed_point(rows):
    scale = 1
    while scale * 2 * clip_bound * rows <= 32000:
        scale *= 2
    return float(scale)


def kernel(
    n, nv, rows, texts, pos, width, piece, win,
    owner, counts, tokens, priv, pub, noise,
    combined_out, stats_out,
    pv, xt, pubf, pubs, here, pref, keep, snd1, rs1, snd2, rs2,
    hist, st1, st2, bnd, order, sown, start,
    priv_sem, hist_s, hist_r, ag_s, ag_f, ag_r, rs1_s, rs1_r, rs2_s, rs2_r,
    st1_s, st1_r, st2_s, st2_r,
):
    f32 = jnp.float32
    half = n // 2
    full = width // LANES
    wl = win * LANES
    me = lax.axis_index("ref")
    mv = lax.axis_index("voc")
    z = lax.div(me, 2)
    x = lax.rem(me, 2)
    partner = me + 1 - 2 * x
    scale1 = fixed_point(rows)
    scale2 = fixed_point(2 * rows)

    def first_tile(j):
        return jnp.minimum(lax.div(j * piece, LANES), full + 1 - win)

    def remote(src, dst, send, recv, peer):
        return pltpu.make_async_remote_copy(
            src_ref=src, dst_ref=dst, send_sem=send, recv_sem=recv,
            device_id=peer, device_id_type=MESH,
        )

    load = pltpu.make_async_copy(priv, pv, priv_sem)
    load.start()
    barrier = pltpu.get_barrier_semaphore()

    def greet(k, c):
        pl.semaphore_signal(barrier, inc=1, device_id={"ref": lax.rem(me + k, n)}, device_id_type=MESH)
        return c

    def greet_voc(k, c):
        pl.semaphore_signal(barrier, inc=1, device_id={"voc": lax.rem(mv + k, nv)}, device_id_type=MESH)
        return c

    lax.fori_loop(1, n, greet, 0)
    lax.fori_loop(1, nv, greet_voc, 0)

    shift = me * piece - first_tile(me) * LANES
    pubf[...] = jnp.zeros_like(pubf)
    for t in range(texts):
        pubf[t, :, :piece] = pub[t].astype(f32)
    for t in range(texts):
        pubs[me, t] = pltpu.roll(pubf[t], shift, 1).astype(jnp.bfloat16)

    own = [owner[r] for r in range(rows)]
    hits = [sum((o == t).astype(jnp.int32) for o in own) for t in range(texts)]
    lane8 = lax.broadcasted_iota(jnp.int32, (8, LANES), 1)
    mine = jnp.zeros((8, LANES), jnp.int32)
    for t in range(texts):
        mine = jnp.where(lane8 == t, hits[t], mine)
    hist[me] = mine

    pl.semaphore_wait(barrier, n - 1 + nv - 1)

    def send_hist(k, c):
        remote(hist.at[me], hist.at[me], hist_s, hist_r, {"ref": lax.rem(me + k, n)}).start()
        return c

    lax.fori_loop(1, n, send_hist, 0)
    remote(pubs.at[me], pubs.at[me], ag_s.at[0], ag_r.at[me], {"ref": partner}).start()

    def send_own(k, c):
        peer = 2 * lax.rem(z + k, half) + x
        remote(pubs.at[me], pubs.at[me], ag_s.at[k], ag_r.at[me], {"ref": peer}).start()
        return c

    lax.fori_loop(1, half, send_own, 0)

    begin = [jnp.int32(0)]
    for t in range(texts):
        begin.append(begin[-1] + hits[t])
    for t in range(texts + 1):
        start[t] = begin[t]
    place = []
    for r in range(rows):
        before = jnp.int32(0)
        for q in range(rows):
            if q < r:
                before = before + (own[q] <= own[r]).astype(jnp.int32)
            elif q > r:
                before = before + (own[q] < own[r]).astype(jnp.int32)
        place.append(before)
    for k in range(rows):
        at = jnp.int32(0)
        for r in range(rows):
            at = at + jnp.where(place[r] == k, r, 0)
        order[k] = at
        sown[k] = sum((begin[t] <= k).astype(jnp.int32) for t in range(1, texts))

    load.wait()
    for j in range(n):
        s = min(j * piece // LANES, full + 1 - win) + win - 1
        if s < full:
            xt[:, :, j * LANES:(j + 1) * LANES] = pv[:, :, s * LANES:(s + 1) * LANES]
        else:
            xt[:, :, j * LANES:(j + 1) * LANES] = jnp.zeros((rows, pos, LANES), jnp.bfloat16)
            if width > full * LANES:
                xt[:, :, j * LANES:j * LANES + width - full * LANES] = pv[:, :, full * LANES:]

    got = hist.at[pl.ds(0, n - 1)]
    pltpu.make_async_copy(got, got, hist_r).wait()
    pltpu.make_async_copy(got, got, hist_s).wait()
    lower = jnp.zeros((8, LANES), jnp.int32)
    lower = lax.fori_loop(0, n, lambda j, a: a + jnp.where(j < me, hist[j], 0), lower)
    lower = lower[:pos]
    lane4 = lax.broadcasted_iota(jnp.int32, (pos, LANES), 1)
    for k in range(rows):
        text = sown[k]
        limit = counts[text] - (k - start[text])
        ok = jnp.where((lane4 == text) & (lower < limit), clip_bound, 0.0)
        bnd[k] = jnp.broadcast_to(jnp.max(ok, axis=1, keepdims=True), (pos, LANES))

    tiles = max(c for c in range(1, 9) if (win - 1) % c == 0)

    def partial_sums(j, store):
        base = first_tile(j)
        for t in range(texts):
            here[t] = pubs[j, t].astype(f32)

        def some(count, source, at, to):
            acc = [jnp.zeros((pos, LANES), f32)] * count
            for c in range(count):
                pref[0, :, c * LANES:(c + 1) * LANES] = acc[c]
            for k in range(rows):
                row = order[k]
                text = sown[k]
                b = bnd[k]
                for c in range(count):
                    p = source[row, :, pl.ds(pl.multiple_of(at + c * LANES, LANES), LANES)].astype(f32)
                    u = here[text, :, pl.ds(pl.multiple_of(to + c * LANES, LANES), LANES)]
                    acc[c] = acc[c] + jnp.minimum(jnp.maximum(p - u, -b), b)
                    pref[k + 1, :, c * LANES:(c + 1) * LANES] = acc[c]
            for t in range(texts):
                v = pref[start[t + 1], :, :count * LANES] - pref[start[t], :, :count * LANES]
                store(t, pl.ds(pl.multiple_of(to, LANES), count * LANES), v)

        def chunk(i, c):
            to = i * (tiles * LANES)
            some(tiles, pv, base * LANES + to, to)
            return c

        lax.fori_loop(0, (win - 1) // tiles, chunk, 0)
        some(1, xt, j * LANES, (win - 1) * LANES)

    def coded(v, scale):
        return jnp.round(v * scale).astype(jnp.int32).astype(jnp.int16)

    def decoded(q, scale):
        return q.astype(jnp.int32).astype(f32) * (1.0 / scale)

    def column(i):
        return lax.rem(z - i + half, half)

    def step(i, c):
        @pl.when(i < half)
        def _():
            zi = column(i)
            j = 2 * zi + x

            @pl.when(i > 0)
            def _():
                remote(pubs.at[j], pubs.at[j], ag_f.at[zi], ag_r.at[j], {"ref": partner}).wait_recv()
                remote(pubs.at[j], pubs.at[j], ag_f.at[zi], ag_r.at[j], {"ref": partner}).start()

            def store(t, lanes, v):
                keep[zi, t, :, lanes] = v

            partial_sums(j, store)

        @pl.when((i >= 1) & (i <= half))
        def _():
            zi = column(i - 1)
            j = 2 * zi + 1 - x
            remote(pubs.at[j], pubs.at[j], ag_f.at[zi], ag_r.at[j], {"ref": partner}).wait_recv()

            def store(t, lanes, v):
                snd1[zi, t, :, lanes] = coded(v, scale1)

            partial_sums(j, store)
            remote(snd1.at[zi], rs1.at[zi], rs1_s.at[zi], rs1_r.at[zi], {"ref": partner}).start()

        @pl.when(i >= 2)
        def _():
            zi = column(i - 2)
            remote(snd1.at[zi], rs1.at[zi], rs1_s.at[zi], rs1_r.at[zi], {"ref": partner}).wait_recv()

            @pl.when(i == 2)
            def _():
                for t in range(texts):
                    keep[zi, t] = keep[zi, t] + decoded(rs1[zi, t], scale1)

            @pl.when(i > 2)
            def _():
                for t in range(texts):
                    snd2[zi, t] = coded(keep[zi, t] + decoded(rs1[zi, t], scale1), scale2)
                remote(snd2.at[zi], rs2.at[z], rs2_s.at[zi], rs2_r.at[z], {"ref": 2 * zi + x}).start()

        return c

    lax.fori_loop(0, half + 2, step, 0)

    def gather(k, c):
        zi = lax.rem(z + k, half)
        remote(snd2.at[zi], rs2.at[zi], rs2_s.at[zi], rs2_r.at[zi], {"ref": 2 * zi + x}).wait_recv()
        for t in range(texts):
            keep[z, t] = keep[z, t] + decoded(rs2[zi, t], scale2)
        return c

    lax.fori_loop(1, half, gather, 0)

    first_column = (mv * n + me) * piece
    at_column = lax.broadcasted_iota(jnp.int32, (pos, piece), 1) + first_column
    at_pos = lax.broadcasted_iota(jnp.int32, (pos, 1), 0)
    lse_all = jnp.zeros((pos, LANES), f32)
    picked_all = jnp.zeros((pos, LANES), f32)
    for t in range(texts):
        summed = pltpu.roll(keep[z, t], lax.rem(wl - shift, wl), 1)[:, :piece]
        root = jnp.sqrt(jnp.full((pos, LANES), counts[t].astype(f32), f32))
        factor = (1.0 / (clip_bound * root))[:, :1]
        combined = pub[t].astype(f32) + summed * factor + noise[t].astype(f32)
        combined_out[t] = combined
        peak = jnp.max(combined, axis=1, keepdims=True)
        total = jnp.sum(jnp.exp(combined - peak), axis=1, keepdims=True)
        token = jnp.zeros((pos, 1), jnp.int32)
        for p in range(pos):
            token = jnp.where(at_pos == p, tokens[t, p], token)
        picked = jnp.sum(jnp.where(at_column == token, combined, 0.0), axis=1, keepdims=True)
        lse_all = jnp.where(lane4 == t, peak + jnp.log(total), lse_all)
        picked_all = jnp.where(lane4 == t, picked, picked_all)

    def exchange(slots, send, recv, index, count, axis, lse, picked):
        slots[index, :pos] = lse
        slots[index, pos:2 * pos] = picked

        def send_one(k, c):
            remote(slots.at[index], slots.at[index], send, recv, {axis: lax.rem(index + k, count)}).start()
            return c

        lax.fori_loop(1, count, send_one, 0)
        others = slots.at[pl.ds(0, count - 1)]
        pltpu.make_async_copy(others, others, recv).wait()
        pltpu.make_async_copy(others, others, send).wait()
        top = lax.fori_loop(1, count, lambda j, a: jnp.maximum(a, slots[j, :pos]), slots[0, :pos])
        zero = jnp.zeros((pos, LANES), f32)
        total, found = lax.fori_loop(
            0, count,
            lambda j, a: (a[0] + jnp.exp(slots[j, :pos] - top), a[1] + slots[j, pos:2 * pos]),
            (zero, zero),
        )
        return top + jnp.log(total), found

    lse, picked = exchange(st1, st1_s, st1_r, mv, nv, "voc", lse_all, picked_all)
    lse, picked = exchange(st2, st2_s, st2_r, me, n, "ref", lse, picked)
    stats_out[0] = lse
    stats_out[1] = picked

    def sent(i, c):
        remote(pubs.at[me], pubs.at[me], ag_s.at[i], ag_r.at[me], {"ref": partner}).wait_send()
        remote(snd1.at[i], rs1.at[i], rs1_s.at[i], rs1_r.at[i], {"ref": partner}).wait_send()

        @pl.when(i != z)
        def _():
            remote(pubs.at[me], pubs.at[me], ag_f.at[i], ag_r.at[me], {"ref": partner}).wait_send()
            remote(snd2.at[i], rs2.at[i], rs2_s.at[i], rs2_r.at[i], {"ref": partner}).wait_send()

        return c

    lax.fori_loop(0, half, sent, 0)


def finish(texts, pos, combined, stats, logprobs, target):
    lse = stats[0]
    score = stats[1] - lse
    at_pos = lax.broadcasted_iota(jnp.int32, (pos, pos), 0)
    at_lane = lax.broadcasted_iota(jnp.int32, (pos, pos), 1)
    for t in range(texts):
        logprobs[t] = combined[t] - lse[:, t:t + 1]
        column = jnp.where(at_pos == at_lane, score[:, t:t + 1], 0.0)
        target[t:t + 1, :] = jnp.sum(column, axis=0, keepdims=True)


def body(n, nv, private_logits, public_logits, noise, owner, counts, tokens):
    rows, pos, width = private_logits.shape
    texts, _, piece = public_logits.shape
    half = n // 2
    full = width // LANES
    win = max(-(-((j * piece) % LANES + piece) // LANES) for j in range(n))
    while min(j * piece - LANES * min(j * piece // LANES, full + 1 - win) for j in range(n)) < 0:
        win += 1
    wl = win * LANES
    bf16, f32, i16 = jnp.bfloat16, jnp.float32, jnp.int16
    smem = pl.BlockSpec(memory_space=pltpu.SMEM)
    vmem = pl.BlockSpec(memory_space=pltpu.VMEM)
    dma = pltpu.SemaphoreType.DMA
    combined, stats = pl.pallas_call(
        functools.partial(kernel, n, nv, rows, texts, pos, width, piece, win),
        out_shape=(
            jax.ShapeDtypeStruct((texts, pos, piece), f32),
            jax.ShapeDtypeStruct((2, pos, LANES), f32),
        ),
        in_specs=[smem, smem, smem, pl.BlockSpec(memory_space=pl.ANY), vmem, vmem],
        out_specs=(vmem, vmem),
        scratch_shapes=[
            pltpu.VMEM((rows, pos, width), bf16),
            pltpu.VMEM((rows, pos, n * LANES), bf16),
            pltpu.VMEM((texts, pos, wl), f32),
            pltpu.VMEM((n, texts, pos, wl), bf16),
            pltpu.VMEM((texts, pos, wl), f32),
            pltpu.VMEM((rows + 1, pos, 8 * LANES), f32),
            pltpu.VMEM((half, texts, pos, wl), f32),
            pltpu.VMEM((half, texts, pos, wl), i16),
            pltpu.VMEM((half, texts, pos, wl), i16),
            pltpu.VMEM((half, texts, pos, wl), i16),
            pltpu.VMEM((half, texts, pos, wl), i16),
            pltpu.VMEM((n, 8, LANES), jnp.int32),
            pltpu.VMEM((nv, 2 * pos, LANES), f32),
            pltpu.VMEM((n, 2 * pos, LANES), f32),
            pltpu.VMEM((rows, pos, LANES), f32),
            pltpu.SMEM((rows,), jnp.int32),
            pltpu.SMEM((rows,), jnp.int32),
            pltpu.SMEM((texts + 1,), jnp.int32),
            dma, dma, dma,
            dma((half,)), dma((half,)), dma((n,)),
            dma((half,)), dma((half,)), dma((half,)), dma((half,)),
            dma, dma, dma, dma,
        ],
        compiler_params=pltpu.CompilerParams(
            collective_id=0, has_side_effects=True, vmem_limit_bytes=56 * 1024 * 1024
        ),
        cost_estimate=pl.CostEstimate(
            flops=6 * rows * pos * width, bytes_accessed=2 * rows * pos * width, transcendentals=0
        ),
        name="private_scores",
    )(owner, counts, tokens, private_logits, public_logits, noise)
    return pl.pallas_call(
        functools.partial(finish, texts, pos),
        out_shape=(
            jax.ShapeDtypeStruct((texts, pos, piece), f32),
            jax.ShapeDtypeStruct((texts, pos), f32),
        ),
        in_specs=[vmem, vmem],
        out_specs=(vmem, vmem),
        name="subtract_lse",
    )(combined, stats)


def solution(mesh):
    return jax.shard_map(
        functools.partial(body, mesh.shape["ref"], mesh.shape["voc"]),
        mesh=mesh,
        in_specs=(
            P("ref", None, "voc"),
            P(None, None, ("voc", "ref")),
            P(None, None, ("voc", "ref")),
            P("ref"),
            P(),
            P(),
        ),
        out_specs=(P(None, None, ("voc", "ref")), P()),
        check_vma=False,
    )
```

```python
import functools

import jax
import jax.numpy as jnp
from jax import lax
from jax.experimental import pallas as pl
from jax.experimental.pallas import tpu as pltpu
from jax.sharding import PartitionSpec as P

clip_bound = 2.0
LANES = 128
MESH = pl.DeviceIdType.MESH


def fixed_point(rows):
    scale = 1
    while scale * 2 * clip_bound * rows <= 32000:
        scale *= 2
    return float(scale)


def kernel(
    n, nv, rows, texts, pos, width, piece, win,
    owner, counts, tokens, priv, pub, noise,
    combined_out, stats_out,
    pv, xt, pubf, pubs, here, pref, keep, snd1, rs1, snd2, rs2,
    hist, st1, st2, bnd, order, sown, start,
    priv_sem, hist_s, hist_r, ag_x, ag_up, ag_dn, ag_r, rs1_s, rs1_r, rs2_s, rs2_r,
    st1_s, st1_r, st2_s, st2_r,
):
    f32 = jnp.float32
    half = n // 2
    full = width // LANES
    wl = win * LANES
    me = lax.axis_index("ref")
    mv = lax.axis_index("voc")
    z = lax.div(me, 2)
    x = lax.rem(me, 2)
    partner = me + 1 - 2 * x
    scale1 = fixed_point(rows)
    scale2 = fixed_point(2 * rows)

    def first_tile(j):
        return jnp.minimum(lax.div(j * piece, LANES), full + 1 - win)

    def remote(src, dst, send, recv, peer):
        return pltpu.make_async_remote_copy(
            src_ref=src, dst_ref=dst, send_sem=send, recv_sem=recv,
            device_id=peer, device_id_type=MESH,
        )

    load = pltpu.make_async_copy(priv, pv, priv_sem)
    load.start()
    barrier = pltpu.get_barrier_semaphore()

    def greet(k, c):
        pl.semaphore_signal(barrier, inc=1, device_id={"ref": lax.rem(me + k, n)}, device_id_type=MESH)
        return c

    def greet_voc(k, c):
        pl.semaphore_signal(barrier, inc=1, device_id={"voc": lax.rem(mv + k, nv)}, device_id_type=MESH)
        return c

    lax.fori_loop(1, n, greet, 0)
    lax.fori_loop(1, nv, greet_voc, 0)

    shift = me * piece - first_tile(me) * LANES
    pubf[...] = jnp.zeros_like(pubf)
    for t in range(texts):
        pubf[t, :, :piece] = pub[t].astype(f32)
    for t in range(texts):
        pubs[me, t] = pltpu.roll(pubf[t], shift, 1).astype(jnp.bfloat16)

    own = [owner[r] for r in range(rows)]
    hits = [sum((o == t).astype(jnp.int32) for o in own) for t in range(texts)]
    lane8 = lax.broadcasted_iota(jnp.int32, (8, LANES), 1)
    mine = jnp.zeros((8, LANES), jnp.int32)
    for t in range(texts):
        mine = jnp.where(lane8 == t, hits[t], mine)
    hist[me] = mine

    pl.semaphore_wait(barrier, n - 1 + nv - 1)

    def pass_on(zi):
        j = 2 * zi + x
        remote(pubs.at[j], pubs.at[j], ag_x.at[zi], ag_r.at[j], {"ref": partner}).start()

        @pl.when((zi <= z) & (z < half - 1))
        def _():
            remote(pubs.at[j], pubs.at[j], ag_up.at[zi], ag_r.at[j], {"ref": me + 2}).start()

        @pl.when((zi >= z) & (z > 0))
        def _():
            remote(pubs.at[j], pubs.at[j], ag_dn.at[zi], ag_r.at[j], {"ref": me - 2}).start()

    pass_on(z)

    def send_hist(k, c):
        remote(hist.at[me], hist.at[me], hist_s, hist_r, {"ref": lax.rem(me + k, n)}).start()
        return c

    lax.fori_loop(1, n, send_hist, 0)
    begin = [jnp.int32(0)]
    for t in range(texts):
        begin.append(begin[-1] + hits[t])
    for t in range(texts + 1):
        start[t] = begin[t]
    place = []
    for r in range(rows):
        before = jnp.int32(0)
        for q in range(rows):
            if q < r:
                before = before + (own[q] <= own[r]).astype(jnp.int32)
            elif q > r:
                before = before + (own[q] < own[r]).astype(jnp.int32)
        place.append(before)
    for k in range(rows):
        at = jnp.int32(0)
        for r in range(rows):
            at = at + jnp.where(place[r] == k, r, 0)
        order[k] = at
        sown[k] = sum((begin[t] <= k).astype(jnp.int32) for t in range(1, texts))

    load.wait()
    for j in range(n):
        s = min(j * piece // LANES, full + 1 - win) + win - 1
        if s < full:
            xt[:, :, j * LANES:(j + 1) * LANES] = pv[:, :, s * LANES:(s + 1) * LANES]
        else:
            xt[:, :, j * LANES:(j + 1) * LANES] = jnp.zeros((rows, pos, LANES), jnp.bfloat16)
            if width > full * LANES:
                xt[:, :, j * LANES:j * LANES + width - full * LANES] = pv[:, :, full * LANES:]

    got = hist.at[pl.ds(0, n - 1)]
    pltpu.make_async_copy(got, got, hist_r).wait()
    pltpu.make_async_copy(got, got, hist_s).wait()
    lower = jnp.zeros((8, LANES), jnp.int32)
    lower = lax.fori_loop(0, n, lambda j, a: a + jnp.where(j < me, hist[j], 0), lower)
    lower = lower[:pos]
    lane4 = lax.broadcasted_iota(jnp.int32, (pos, LANES), 1)
    for k in range(rows):
        text = sown[k]
        limit = counts[text] - (k - start[text])
        ok = jnp.where((lane4 == text) & (lower < limit), clip_bound, 0.0)
        bnd[k] = jnp.broadcast_to(jnp.max(ok, axis=1, keepdims=True), (pos, LANES))

    tiles = max(c for c in range(1, 9) if (win - 1) % c == 0)

    def partial_sums(j, store):
        base = first_tile(j)
        for t in range(texts):
            here[t] = pubs[j, t].astype(f32)

        def some(count, source, at, to):
            acc = [jnp.zeros((pos, LANES), f32)] * count
            for c in range(count):
                pref[0, :, c * LANES:(c + 1) * LANES] = acc[c]
            for k in range(rows):
                row = order[k]
                text = sown[k]
                b = bnd[k]
                for c in range(count):
                    p = source[row, :, pl.ds(pl.multiple_of(at + c * LANES, LANES), LANES)].astype(f32)
                    u = here[text, :, pl.ds(pl.multiple_of(to + c * LANES, LANES), LANES)]
                    acc[c] = acc[c] + jnp.minimum(jnp.maximum(p - u, -b), b)
                    pref[k + 1, :, c * LANES:(c + 1) * LANES] = acc[c]
            for t in range(texts):
                v = pref[start[t + 1], :, :count * LANES] - pref[start[t], :, :count * LANES]
                store(t, pl.ds(pl.multiple_of(to, LANES), count * LANES), v)

        def chunk(i, c):
            to = i * (tiles * LANES)
            some(tiles, pv, base * LANES + to, to)
            return c

        lax.fori_loop(0, (win - 1) // tiles, chunk, 0)
        some(1, xt, j * LANES, (win - 1) * LANES)

    def coded(v, scale):
        return jnp.round(v * scale).astype(jnp.int32).astype(jnp.int16)

    def decoded(q, scale):
        return q.astype(jnp.int32).astype(f32) * (1.0 / scale)

    nearer = jnp.minimum(z, half - 1 - z)

    def column(i):
        side = jnp.where(lax.rem(i, 2) == 1, -lax.div(i + 1, 2), lax.div(i, 2))
        rest = jnp.where(z < half - 1 - z, i, half - 1 - i)
        return jnp.where(i <= 2 * nearer, z + side, rest)

    def own_column(i):
        zi = column(i)

        def store(t, lanes, v):
            keep[zi, t, :, lanes] = v

        partial_sums(2 * zi + x, store)

    def arrive(i, c):
        zi = column(i)
        j = 2 * zi + x
        remote(pubs.at[j], pubs.at[j], ag_x.at[zi], ag_r.at[j], {"ref": partner}).wait_recv()
        pass_on(zi)

        @pl.when(i >= 2)
        def _():
            own_column(i - 1)

        return c

    def other_column(i, c):
        zi = column(lax.rem(i, half))
        j = 2 * zi + 1 - x
        remote(pubs.at[j], pubs.at[j], ag_x.at[zi], ag_r.at[j], {"ref": partner}).wait_recv()

        def store(t, lanes, v):
            snd1[zi, t, :, lanes] = coded(v, scale1)

        partial_sums(j, store)
        remote(snd1.at[zi], rs1.at[zi], rs1_s.at[zi], rs1_r.at[zi], {"ref": partner}).start()
        return c

    def add_partner(i, c):
        zi = column(lax.rem(i, half))
        remote(snd1.at[zi], rs1.at[zi], rs1_s.at[zi], rs1_r.at[zi], {"ref": partner}).wait_recv()

        @pl.when(i == half)
        def _():
            for t in range(texts):
                keep[zi, t] = keep[zi, t] + decoded(rs1[zi, t], scale1)

        @pl.when(i < half)
        def _():
            for t in range(texts):
                snd2[zi, t] = coded(keep[zi, t] + decoded(rs1[zi, t], scale1), scale2)
            remote(snd2.at[zi], rs2.at[z], rs2_s.at[zi], rs2_r.at[z], {"ref": 2 * zi + x}).start()

        return c

    own_column(jnp.int32(0))
    lax.fori_loop(1, half, arrive, 0)
    lax.fori_loop(1, half + 1, other_column, 0)
    own_column(jnp.int32(half - 1))
    lax.fori_loop(1, half + 1, add_partner, 0)

    def gather(k, c):
        zi = lax.rem(z + k, half)
        remote(snd2.at[zi], rs2.at[zi], rs2_s.at[zi], rs2_r.at[zi], {"ref": 2 * zi + x}).wait_recv()
        for t in range(texts):
            keep[z, t] = keep[z, t] + decoded(rs2[zi, t], scale2)
        return c

    lax.fori_loop(1, half, gather, 0)

    first_column = (mv * n + me) * piece
    at_column = lax.broadcasted_iota(jnp.int32, (pos, piece), 1) + first_column
    at_pos = lax.broadcasted_iota(jnp.int32, (pos, 1), 0)
    lse_all = jnp.zeros((pos, LANES), f32)
    picked_all = jnp.zeros((pos, LANES), f32)
    for t in range(texts):
        summed = pltpu.roll(keep[z, t], lax.rem(wl - shift, wl), 1)[:, :piece]
        root = jnp.sqrt(jnp.full((pos, LANES), counts[t].astype(f32), f32))
        factor = (1.0 / (clip_bound * root))[:, :1]
        combined = pub[t].astype(f32) + summed * factor + noise[t].astype(f32)
        combined_out[t] = combined
        peak = jnp.max(combined, axis=1, keepdims=True)
        total = jnp.sum(jnp.exp(combined - peak), axis=1, keepdims=True)
        token = jnp.zeros((pos, 1), jnp.int32)
        for p in range(pos):
            token = jnp.where(at_pos == p, tokens[t, p], token)
        picked = jnp.sum(jnp.where(at_column == token, combined, 0.0), axis=1, keepdims=True)
        lse_all = jnp.where(lane4 == t, peak + jnp.log(total), lse_all)
        picked_all = jnp.where(lane4 == t, picked, picked_all)

    def exchange(slots, send, recv, index, count, axis, lse, picked):
        slots[index, :pos] = lse
        slots[index, pos:2 * pos] = picked

        def send_one(k, c):
            remote(slots.at[index], slots.at[index], send, recv, {axis: lax.rem(index + k, count)}).start()
            return c

        lax.fori_loop(1, count, send_one, 0)
        others = slots.at[pl.ds(0, count - 1)]
        pltpu.make_async_copy(others, others, recv).wait()
        pltpu.make_async_copy(others, others, send).wait()
        top = lax.fori_loop(1, count, lambda j, a: jnp.maximum(a, slots[j, :pos]), slots[0, :pos])
        zero = jnp.zeros((pos, LANES), f32)
        total, found = lax.fori_loop(
            0, count,
            lambda j, a: (a[0] + jnp.exp(slots[j, :pos] - top), a[1] + slots[j, pos:2 * pos]),
            (zero, zero),
        )
        return top + jnp.log(total), found

    lse, picked = exchange(st1, st1_s, st1_r, mv, nv, "voc", lse_all, picked_all)
    lse, picked = exchange(st2, st2_s, st2_r, me, n, "ref", lse, picked)
    stats_out[0] = lse
    stats_out[1] = picked

    def sent(i, c):
        remote(pubs.at[me], pubs.at[me], ag_x.at[i], ag_r.at[me], {"ref": partner}).wait_send()
        remote(snd1.at[i], rs1.at[i], rs1_s.at[i], rs1_r.at[i], {"ref": partner}).wait_send()

        @pl.when((i <= z) & (z < half - 1))
        def _():
            remote(pubs.at[me], pubs.at[me], ag_up.at[i], ag_r.at[me], {"ref": partner}).wait_send()

        @pl.when((i >= z) & (z > 0))
        def _():
            remote(pubs.at[me], pubs.at[me], ag_dn.at[i], ag_r.at[me], {"ref": partner}).wait_send()

        @pl.when(i != z)
        def _():
            remote(snd2.at[i], rs2.at[i], rs2_s.at[i], rs2_r.at[i], {"ref": partner}).wait_send()

        return c

    lax.fori_loop(0, half, sent, 0)


def finish(texts, pos, combined, stats, logprobs, target):
    lse = stats[0]
    score = stats[1] - lse
    at_pos = lax.broadcasted_iota(jnp.int32, (pos, pos), 0)
    at_lane = lax.broadcasted_iota(jnp.int32, (pos, pos), 1)
    for t in range(texts):
        logprobs[t] = combined[t] - lse[:, t:t + 1]
        column = jnp.where(at_pos == at_lane, score[:, t:t + 1], 0.0)
        target[t:t + 1, :] = jnp.sum(column, axis=0, keepdims=True)


def body(n, nv, private_logits, public_logits, noise, owner, counts, tokens):
    rows, pos, width = private_logits.shape
    texts, _, piece = public_logits.shape
    half = n // 2
    full = width // LANES
    win = max(-(-((j * piece) % LANES + piece) // LANES) for j in range(n))
    while min(j * piece - LANES * min(j * piece // LANES, full + 1 - win) for j in range(n)) < 0:
        win += 1
    wl = win * LANES
    bf16, f32, i16 = jnp.bfloat16, jnp.float32, jnp.int16
    smem = pl.BlockSpec(memory_space=pltpu.SMEM)
    vmem = pl.BlockSpec(memory_space=pltpu.VMEM)
    dma = pltpu.SemaphoreType.DMA
    combined, stats = pl.pallas_call(
        functools.partial(kernel, n, nv, rows, texts, pos, width, piece, win),
        out_shape=(
            jax.ShapeDtypeStruct((texts, pos, piece), f32),
            jax.ShapeDtypeStruct((2, pos, LANES), f32),
        ),
        in_specs=[smem, smem, smem, pl.BlockSpec(memory_space=pl.ANY), vmem, vmem],
        out_specs=(vmem, vmem),
        scratch_shapes=[
            pltpu.VMEM((rows, pos, width), bf16),
            pltpu.VMEM((rows, pos, n * LANES), bf16),
            pltpu.VMEM((texts, pos, wl), f32),
            pltpu.VMEM((n, texts, pos, wl), bf16),
            pltpu.VMEM((texts, pos, wl), f32),
            pltpu.VMEM((rows + 1, pos, 8 * LANES), f32),
            pltpu.VMEM((half, texts, pos, wl), f32),
            pltpu.VMEM((half, texts, pos, wl), i16),
            pltpu.VMEM((half, texts, pos, wl), i16),
            pltpu.VMEM((half, texts, pos, wl), i16),
            pltpu.VMEM((half, texts, pos, wl), i16),
            pltpu.VMEM((n, 8, LANES), jnp.int32),
            pltpu.VMEM((nv, 2 * pos, LANES), f32),
            pltpu.VMEM((n, 2 * pos, LANES), f32),
            pltpu.VMEM((rows, pos, LANES), f32),
            pltpu.SMEM((rows,), jnp.int32),
            pltpu.SMEM((rows,), jnp.int32),
            pltpu.SMEM((texts + 1,), jnp.int32),
            dma, dma, dma,
            dma((half,)), dma((half,)), dma((half,)), dma((n,)),
            dma((half,)), dma((half,)), dma((half,)), dma((half,)),
            dma, dma, dma, dma,
        ],
        compiler_params=pltpu.CompilerParams(
            collective_id=0, has_side_effects=True, vmem_limit_bytes=56 * 1024 * 1024
        ),
        cost_estimate=pl.CostEstimate(
            flops=6 * rows * pos * width, bytes_accessed=2 * rows * pos * width, transcendentals=0
        ),
        name="private_scores",
    )(owner, counts, tokens, private_logits, public_logits, noise)
    return pl.pallas_call(
        functools.partial(finish, texts, pos),
        out_shape=(
            jax.ShapeDtypeStruct((texts, pos, piece), f32),
            jax.ShapeDtypeStruct((texts, pos), f32),
        ),
        in_specs=[vmem, vmem],
        out_specs=(vmem, vmem),
        name="subtract_lse",
    )(combined, stats)


def solution(mesh):
    return jax.shard_map(
        functools.partial(body, mesh.shape["ref"], mesh.shape["voc"]),
        mesh=mesh,
        in_specs=(
            P("ref", None, "voc"),
            P(None, None, ("voc", "ref")),
            P(None, None, ("voc", "ref")),
            P("ref"),
            P(),
            P(),
        ),
        out_specs=(P(None, None, ("voc", "ref")), P()),
        check_vma=False,
    )
```

```python
import functools

import jax
import jax.numpy as jnp
from jax import lax
from jax.experimental import pallas as pl
from jax.experimental.pallas import tpu as pltpu
from jax.sharding import PartitionSpec as P

clip_bound = 2.0
LANES = 128
MESH = pl.DeviceIdType.MESH


def fixed_point(rows):
    scale = 1
    while scale * 2 * clip_bound * rows <= 32000:
        scale *= 2
    return float(scale)


def kernel(
    n, nv, rows, texts, pos, width, piece, win,
    owner, counts, tokens, priv, pub, noise,
    combined_out, stats_out,
    pv, xt, pubf, pubs, here, pref, keep, snd1, rs1, snd2, rs2,
    hist, st1, st2, bnd, order, sown, start,
    priv_sem, hist_s, hist_r, ag_x, ag_up, ag_dn, ag_r, rs1_s, rs1_r, rs2_s, rs2_r,
    st1_s, st1_r, st2_s, st2_r,
):
    f32 = jnp.float32
    half = n // 2
    full = width // LANES
    wl = win * LANES
    pairs = win // 2
    hl = pairs * LANES
    me = lax.axis_index("ref")
    mv = lax.axis_index("voc")
    z = lax.div(me, 2)
    x = lax.rem(me, 2)
    partner = me + 1 - 2 * x
    scale1 = fixed_point(rows)
    scale2 = fixed_point(2 * rows)

    def first_tile(j):
        return jnp.minimum(lax.div(j * piece, LANES), full + 1 - win)

    def remote(src, dst, send, recv, peer):
        return pltpu.make_async_remote_copy(
            src_ref=src, dst_ref=dst, send_sem=send, recv_sem=recv,
            device_id=peer, device_id_type=MESH,
        )

    load = pltpu.make_async_copy(priv, pv, priv_sem)
    load.start()
    barrier = pltpu.get_barrier_semaphore()

    def greet(k, c):
        pl.semaphore_signal(barrier, inc=1, device_id={"ref": lax.rem(me + k, n)}, device_id_type=MESH)
        return c

    def greet_voc(k, c):
        pl.semaphore_signal(barrier, inc=1, device_id={"voc": lax.rem(mv + k, nv)}, device_id_type=MESH)
        return c

    lax.fori_loop(1, n, greet, 0)
    lax.fori_loop(1, nv, greet_voc, 0)

    shift = me * piece - first_tile(me) * LANES
    pubf[...] = jnp.zeros_like(pubf)
    for t in range(texts):
        pubf[t, :, :piece] = pub[t].astype(f32)
    for t in range(texts):
        moved = pltpu.roll(pubf[t], shift, 1)
        pubs[me, t] = jnp.concatenate([moved[:, :hl], moved[:, hl:]], axis=0).astype(jnp.bfloat16)

    own = [owner[r] for r in range(rows)]
    hits = [sum((o == t).astype(jnp.int32) for o in own) for t in range(texts)]
    lane8 = lax.broadcasted_iota(jnp.int32, (2 * pos, LANES), 1)
    mine = jnp.zeros((2 * pos, LANES), jnp.int32)
    for t in range(texts):
        mine = jnp.where(lane8 == t, hits[t], mine)
    hist[me] = mine

    pl.semaphore_wait(barrier, n - 1 + nv - 1)

    def pass_on(zi):
        j = 2 * zi + x
        remote(pubs.at[j], pubs.at[j], ag_x.at[zi], ag_r.at[j], {"ref": partner}).start()

        @pl.when((zi <= z) & (z < half - 1))
        def _():
            remote(pubs.at[j], pubs.at[j], ag_up.at[zi], ag_r.at[j], {"ref": me + 2}).start()

        @pl.when((zi >= z) & (z > 0))
        def _():
            remote(pubs.at[j], pubs.at[j], ag_dn.at[zi], ag_r.at[j], {"ref": me - 2}).start()

    def send_hist(k, c):
        remote(hist.at[me], hist.at[me], hist_s, hist_r, {"ref": lax.rem(me + k, n)}).start()
        return c

    lax.fori_loop(1, n, send_hist, 0)
    pass_on(z)

    begin = [jnp.int32(0)]
    for t in range(texts):
        begin.append(begin[-1] + hits[t])
    for t in range(texts + 1):
        start[t] = begin[t]
    place = []
    for r in range(rows):
        before = jnp.int32(0)
        for q in range(rows):
            if q < r:
                before = before + (own[q] <= own[r]).astype(jnp.int32)
            elif q > r:
                before = before + (own[q] < own[r]).astype(jnp.int32)
        place.append(before)
    for k in range(rows):
        at = jnp.int32(0)
        for r in range(rows):
            at = at + jnp.where(place[r] == k, r, 0)
        order[k] = at
        sown[k] = sum((begin[t] <= k).astype(jnp.int32) for t in range(1, texts))

    load.wait()
    for j in range(n):
        s = min(j * piece // LANES, full + 1 - win) + win - 1
        if s < full:
            xt[:, :, j * LANES:(j + 1) * LANES] = pv[:, :, s * LANES:(s + 1) * LANES]
        else:
            xt[:, :, j * LANES:(j + 1) * LANES] = jnp.zeros((rows, pos, LANES), jnp.bfloat16)
            if width > full * LANES:
                xt[:, :, j * LANES:j * LANES + width - full * LANES] = pv[:, :, full * LANES:]

    got = hist.at[pl.ds(0, n - 1)]
    pltpu.make_async_copy(got, got, hist_r).wait()
    pltpu.make_async_copy(got, got, hist_s).wait()
    lower = jnp.zeros((2 * pos, LANES), jnp.int32)
    lower = lax.fori_loop(0, n, lambda j, a: a + jnp.where(j < me, hist[j], 0), lower)
    lane4 = lane8[:pos]
    pref[0] = jnp.zeros_like(pref[0])
    for k in range(rows):
        text = sown[k]
        limit = counts[text] - (k - start[text])
        ok = jnp.where((lane8 == text) & (lower < limit), clip_bound, 0.0)
        bnd[k] = jnp.broadcast_to(jnp.max(ok, axis=1, keepdims=True), (2 * pos, LANES))

    def partial_sums(j, store):
        base = first_tile(j) * LANES
        for t in range(texts):
            here[t] = pubs[j, t].astype(f32)
        acc = [jnp.zeros((2 * pos, LANES), f32)] * pairs
        for k in range(rows):
            row = order[k]
            text = sown[k]
            b = bnd[k]
            for c in range(pairs):
                low = pv[row, :, pl.ds(pl.multiple_of(base + c * LANES, LANES), LANES)]
                if c < pairs - 1:
                    high = pv[row, :, pl.ds(pl.multiple_of(base + hl + c * LANES, LANES), LANES)]
                else:
                    high = xt[row, :, pl.ds(pl.multiple_of(j * LANES, LANES), LANES)]
                p = jnp.concatenate([low.astype(f32), high.astype(f32)], axis=0)
                u = here[text, :, c * LANES:(c + 1) * LANES]
                acc[c] = acc[c] + jnp.minimum(jnp.maximum(p - u, -b), b)
                pref[k + 1, :, c * LANES:(c + 1) * LANES] = acc[c]
        for t in range(texts):
            store(t, pref[start[t + 1]] - pref[start[t]])

    def coded(v, scale):
        return jnp.round(v * scale).astype(jnp.int32).astype(jnp.int16)

    def decoded(q, scale):
        return q.astype(jnp.int32).astype(f32) * (1.0 / scale)

    nearer = jnp.minimum(z, half - 1 - z)

    def column(i):
        side = jnp.where(lax.rem(i, 2) == 1, -lax.div(i + 1, 2), lax.div(i, 2))
        rest = jnp.where(z < half - 1 - z, i, half - 1 - i)
        return jnp.where(i <= 2 * nearer, z + side, rest)

    def own_column(i):
        zi = column(i)

        def store(t, v):
            keep[zi, t] = v

        partial_sums(2 * zi + x, store)

    def arrive(i, c):
        zi = column(i)
        j = 2 * zi + x
        remote(pubs.at[j], pubs.at[j], ag_x.at[zi], ag_r.at[j], {"ref": partner}).wait_recv()
        pass_on(zi)

        @pl.when(i >= 2)
        def _():
            own_column(i - 1)

        return c

    def other_column(i, c):
        zi = column(lax.rem(i, half))
        j = 2 * zi + 1 - x
        remote(pubs.at[j], pubs.at[j], ag_x.at[zi], ag_r.at[j], {"ref": partner}).wait_recv()

        def store(t, v):
            snd1[zi, t] = coded(v, scale1)

        partial_sums(j, store)
        remote(snd1.at[zi], rs1.at[zi], rs1_s.at[zi], rs1_r.at[zi], {"ref": partner}).start()
        return c

    def add_partner(i, c):
        zi = column(lax.rem(i, half))
        remote(snd1.at[zi], rs1.at[zi], rs1_s.at[zi], rs1_r.at[zi], {"ref": partner}).wait_recv()

        @pl.when(i == half)
        def _():
            for t in range(texts):
                keep[zi, t] = keep[zi, t] + decoded(rs1[zi, t], scale1)

        @pl.when(i < half)
        def _():
            for t in range(texts):
                snd2[zi, t] = coded(keep[zi, t] + decoded(rs1[zi, t], scale1), scale2)
            remote(snd2.at[zi], rs2.at[z], rs2_s.at[zi], rs2_r.at[z], {"ref": 2 * zi + x}).start()

        return c

    own_column(jnp.int32(0))
    lax.fori_loop(1, half, arrive, 0)
    lax.fori_loop(1, half + 1, other_column, 0)
    own_column(jnp.int32(half - 1))
    lax.fori_loop(1, half + 1, add_partner, 0)

    def gather(k, c):
        zi = lax.rem(z + k, half)
        remote(snd2.at[zi], rs2.at[zi], rs2_s.at[zi], rs2_r.at[zi], {"ref": 2 * zi + x}).wait_recv()
        for t in range(texts):
            keep[z, t] = keep[z, t] + decoded(rs2[zi, t], scale2)
        return c

    lax.fori_loop(1, half, gather, 0)

    first_column = (mv * n + me) * piece
    at_column = lax.broadcasted_iota(jnp.int32, (pos, piece), 1) + first_column
    at_pos = lax.broadcasted_iota(jnp.int32, (pos, 1), 0)
    lse_all = jnp.zeros((pos, LANES), f32)
    picked_all = jnp.zeros((pos, LANES), f32)
    for t in range(texts):
        both = keep[z, t]
        summed = jnp.concatenate([both[:pos], both[pos:]], axis=1)
        summed = pltpu.roll(summed, lax.rem(wl - shift, wl), 1)[:, :piece]
        root = jnp.sqrt(jnp.full((pos, LANES), counts[t].astype(f32), f32))
        factor = (1.0 / (clip_bound * root))[:, :1]
        combined = pub[t].astype(f32) + summed * factor + noise[t].astype(f32)
        combined_out[t] = combined
        peak = jnp.max(combined, axis=1, keepdims=True)
        total = jnp.sum(jnp.exp(combined - peak), axis=1, keepdims=True)
        token = jnp.zeros((pos, 1), jnp.int32)
        for p in range(pos):
            token = jnp.where(at_pos == p, tokens[t, p], token)
        picked = jnp.sum(jnp.where(at_column == token, combined, 0.0), axis=1, keepdims=True)
        lse_all = jnp.where(lane4 == t, peak + jnp.log(total), lse_all)
        picked_all = jnp.where(lane4 == t, picked, picked_all)

    def exchange(slots, send, recv, index, count, axis, lse, picked):
        slots[index, :pos] = lse
        slots[index, pos:2 * pos] = picked

        def send_one(k, c):
            remote(slots.at[index], slots.at[index], send, recv, {axis: lax.rem(index + k, count)}).start()
            return c

        lax.fori_loop(1, count, send_one, 0)
        others = slots.at[pl.ds(0, count - 1)]
        pltpu.make_async_copy(others, others, recv).wait()
        pltpu.make_async_copy(others, others, send).wait()
        top = lax.fori_loop(1, count, lambda j, a: jnp.maximum(a, slots[j, :pos]), slots[0, :pos])
        zero = jnp.zeros((pos, LANES), f32)
        total, found = lax.fori_loop(
            0, count,
            lambda j, a: (a[0] + jnp.exp(slots[j, :pos] - top), a[1] + slots[j, pos:2 * pos]),
            (zero, zero),
        )
        return top + jnp.log(total), found

    lse, picked = exchange(st1, st1_s, st1_r, mv, nv, "voc", lse_all, picked_all)
    lse, picked = exchange(st2, st2_s, st2_r, me, n, "ref", lse, picked)
    stats_out[0] = lse
    stats_out[1] = picked

    def sent(i, c):
        remote(pubs.at[me], pubs.at[me], ag_x.at[i], ag_r.at[me], {"ref": partner}).wait_send()
        remote(snd1.at[i], rs1.at[i], rs1_s.at[i], rs1_r.at[i], {"ref": partner}).wait_send()

        @pl.when((i <= z) & (z < half - 1))
        def _():
            remote(pubs.at[me], pubs.at[me], ag_up.at[i], ag_r.at[me], {"ref": partner}).wait_send()

        @pl.when((i >= z) & (z > 0))
        def _():
            remote(pubs.at[me], pubs.at[me], ag_dn.at[i], ag_r.at[me], {"ref": partner}).wait_send()

        @pl.when(i != z)
        def _():
            remote(snd2.at[i], rs2.at[i], rs2_s.at[i], rs2_r.at[i], {"ref": partner}).wait_send()

        return c

    lax.fori_loop(0, half, sent, 0)


def finish(texts, pos, combined, stats, logprobs, target):
    lse = stats[0]
    score = stats[1] - lse
    at_pos = lax.broadcasted_iota(jnp.int32, (pos, pos), 0)
    at_lane = lax.broadcasted_iota(jnp.int32, (pos, pos), 1)
    for t in range(texts):
        logprobs[t] = combined[t] - lse[:, t:t + 1]
        column = jnp.where(at_pos == at_lane, score[:, t:t + 1], 0.0)
        target[t:t + 1, :] = jnp.sum(column, axis=0, keepdims=True)


def body(n, nv, private_logits, public_logits, noise, owner, counts, tokens):
    rows, pos, width = private_logits.shape
    texts, _, piece = public_logits.shape
    half = n // 2
    full = width // LANES
    win = max(-(-((j * piece) % LANES + piece) // LANES) for j in range(n))
    while min(j * piece - LANES * min(j * piece // LANES, full + 1 - win) for j in range(n)) < 0:
        win += 1
    win += win % 2
    wl = win * LANES
    hl = wl // 2
    bf16, f32, i16 = jnp.bfloat16, jnp.float32, jnp.int16
    smem = pl.BlockSpec(memory_space=pltpu.SMEM)
    vmem = pl.BlockSpec(memory_space=pltpu.VMEM)
    dma = pltpu.SemaphoreType.DMA
    combined, stats = pl.pallas_call(
        functools.partial(kernel, n, nv, rows, texts, pos, width, piece, win),
        out_shape=(
            jax.ShapeDtypeStruct((texts, pos, piece), f32),
            jax.ShapeDtypeStruct((2, pos, LANES), f32),
        ),
        in_specs=[smem, smem, smem, pl.BlockSpec(memory_space=pl.ANY), vmem, vmem],
        out_specs=(vmem, vmem),
        scratch_shapes=[
            pltpu.VMEM((rows, pos, width), bf16),
            pltpu.VMEM((rows, pos, n * LANES), bf16),
            pltpu.VMEM((texts, pos, wl), f32),
            pltpu.VMEM((n, texts, 2 * pos, hl), bf16),
            pltpu.VMEM((texts, 2 * pos, hl), f32),
            pltpu.VMEM((rows + 1, 2 * pos, hl), f32),
            pltpu.VMEM((half, texts, 2 * pos, hl), f32),
            pltpu.VMEM((half, texts, 2 * pos, hl), i16),
            pltpu.VMEM((half, texts, 2 * pos, hl), i16),
            pltpu.VMEM((half, texts, 2 * pos, hl), i16),
            pltpu.VMEM((half, texts, 2 * pos, hl), i16),
            pltpu.VMEM((n, 2 * pos, LANES), jnp.int32),
            pltpu.VMEM((nv, 2 * pos, LANES), f32),
            pltpu.VMEM((n, 2 * pos, LANES), f32),
            pltpu.VMEM((rows, 2 * pos, LANES), f32),
            pltpu.SMEM((rows,), jnp.int32),
            pltpu.SMEM((rows,), jnp.int32),
            pltpu.SMEM((texts + 1,), jnp.int32),
            dma, dma, dma,
            dma((half,)), dma((half,)), dma((half,)), dma((n,)),
            dma((half,)), dma((half,)), dma((half,)), dma((half,)),
            dma, dma, dma, dma,
        ],
        compiler_params=pltpu.CompilerParams(
            collective_id=0, has_side_effects=True, vmem_limit_bytes=56 * 1024 * 1024
        ),
        cost_estimate=pl.CostEstimate(
            flops=6 * rows * pos * width, bytes_accessed=2 * rows * pos * width, transcendentals=0
        ),
        name="private_scores",
    )(owner, counts, tokens, private_logits, public_logits, noise)
    return pl.pallas_call(
        functools.partial(finish, texts, pos),
        out_shape=(
            jax.ShapeDtypeStruct((texts, pos, piece), f32),
            jax.ShapeDtypeStruct((texts, pos), f32),
        ),
        in_specs=[vmem, vmem],
        out_specs=(vmem, vmem),
        name="subtract_lse",
    )(combined, stats)


def solution(mesh):
    return jax.shard_map(
        functools.partial(body, mesh.shape["ref"], mesh.shape["voc"]),
        mesh=mesh,
        in_specs=(
            P("ref", None, "voc"),
            P(None, None, ("voc", "ref")),
            P(None, None, ("voc", "ref")),
            P("ref"),
            P(),
            P(),
        ),
        out_specs=(P(None, None, ("voc", "ref")), P()),
        check_vma=False,
    )
```

```python
import functools

import jax
import jax.numpy as jnp
from jax import lax
from jax.experimental import pallas as pl
from jax.experimental.pallas import tpu as pltpu
from jax.sharding import PartitionSpec as P

clip_bound = 2.0
LANES = 128
MESH = pl.DeviceIdType.MESH


def fixed_point(rows):
    scale = 1
    while scale * 2 * clip_bound * rows <= 32000:
        scale *= 2
    return float(scale)


def turned(pairs):
    return (pairs + 3) // 6


def kernel(
    n, nv, rows, texts, pos, width, piece, win,
    owner, counts, tokens, priv, pub, noise,
    combined_out, stats_out,
    pv, xt, pubf, pubs, here, pref, keep, snd1, rs1, snd2, rs2, rowb, sndb, rsb, sndf, rsf,
    hist, st1, st2, bnd, order, sown, start,
    priv_sem, hist_s, hist_r, ag_x, ag_up, ag_dn, ag_r, agb_up, agb_dn, agb_r,
    rs1_s, rs1_r, rs2_s, rs2_r, rsb_s, rsb_r, rsf_s, rsf_r,
    st1_s, st1_r, st2_s, st2_r,
):
    f32 = jnp.float32
    half = n // 2
    full = width // LANES
    wl = win * LANES
    pairs = win // 2
    hl = pairs * LANES
    hb = turned(pairs) * LANES
    me = lax.axis_index("ref")
    mv = lax.axis_index("voc")
    z = lax.div(me, 2)
    x = lax.rem(me, 2)
    partner = me + 1 - 2 * x
    scale1 = fixed_point(rows)
    scale2 = fixed_point(min(2 * rows, n * rows // texts))
    scale3 = fixed_point(min(half * rows, n * rows // texts))

    def first_tile(j):
        return jnp.minimum(lax.div(j * piece, LANES), full + 1 - win)

    def remote(src, dst, send, recv, peer):
        return pltpu.make_async_remote_copy(
            src_ref=src, dst_ref=dst, send_sem=send, recv_sem=recv,
            device_id=peer, device_id_type=MESH,
        )

    load = pltpu.make_async_copy(priv, pv, priv_sem)
    load.start()
    barrier = pltpu.get_barrier_semaphore()

    def greet(k, c):
        pl.semaphore_signal(barrier, inc=1, device_id={"ref": lax.rem(me + k, n)}, device_id_type=MESH)
        return c

    def greet_voc(k, c):
        pl.semaphore_signal(barrier, inc=1, device_id={"voc": lax.rem(mv + k, nv)}, device_id_type=MESH)
        return c

    lax.fori_loop(1, n, greet, 0)
    lax.fori_loop(1, nv, greet_voc, 0)

    shift = me * piece - first_tile(me) * LANES
    pubf[...] = jnp.zeros_like(pubf)
    for t in range(texts):
        pubf[t, :, :piece] = pub[t].astype(f32)
    for t in range(texts):
        moved = pltpu.roll(pubf[t], shift, 1)
        pubs[me, t] = jnp.concatenate([moved[:, :hl], moved[:, hl:]], axis=0).astype(jnp.bfloat16)

    own = [owner[r] for r in range(rows)]
    hits = [sum((o == t).astype(jnp.int32) for o in own) for t in range(texts)]
    lane8 = lax.broadcasted_iota(jnp.int32, (2 * pos, LANES), 1)
    mine = jnp.zeros((2 * pos, LANES), jnp.int32)
    for t in range(texts):
        mine = jnp.where(lane8 == t, hits[t], mine)
    hist[me] = mine

    pl.semaphore_wait(barrier, n - 1 + nv - 1)

    def whole(j):
        return pubs.at[j]

    def straight(j):
        return pubs.at[j, :, :, pl.ds(hb, hl - hb)]

    def turning(j):
        return pubs.at[j, :, :, pl.ds(0, hb)]

    def to_partner(part, j, zi):
        return remote(part(j), part(j), ag_x.at[zi], ag_r.at[j], {"ref": partner})

    def along(part, j, zi, up, down, recv):
        @pl.when((zi <= z) & (z < half - 1))
        def _():
            remote(part(j), part(j), up.at[zi], recv, {"ref": me + 2}).start()

        @pl.when((zi >= z) & (z > 0))
        def _():
            remote(part(j), part(j), down.at[zi], recv, {"ref": me - 2}).start()

    def pass_turned(zi):
        j = 2 * zi + 1 - x
        along(turning, j, zi, agb_up, agb_dn, agb_r.at[zi])

    def send_hist(k, c):
        remote(hist.at[me], hist.at[me], hist_s, hist_r, {"ref": lax.rem(me + k, n)}).start()
        return c

    lax.fori_loop(1, n, send_hist, 0)
    to_partner(whole, me, z).start()
    along(whole, me, z, ag_up, ag_dn, ag_r.at[me])

    begin = [jnp.int32(0)]
    for t in range(texts):
        begin.append(begin[-1] + hits[t])
    for t in range(texts + 1):
        start[t] = begin[t]
    place = []
    for r in range(rows):
        before = jnp.int32(0)
        for q in range(rows):
            if q < r:
                before = before + (own[q] <= own[r]).astype(jnp.int32)
            elif q > r:
                before = before + (own[q] < own[r]).astype(jnp.int32)
        place.append(before)
    for k in range(rows):
        at = jnp.int32(0)
        for r in range(rows):
            at = at + jnp.where(place[r] == k, r, 0)
        order[k] = at
        sown[k] = sum((begin[t] <= k).astype(jnp.int32) for t in range(1, texts))

    load.wait()
    for j in range(n):
        s = min(j * piece // LANES, full + 1 - win) + win - 1
        if s < full:
            xt[:, :, j * LANES:(j + 1) * LANES] = pv[:, :, s * LANES:(s + 1) * LANES]
        else:
            xt[:, :, j * LANES:(j + 1) * LANES] = jnp.zeros((rows, pos, LANES), jnp.bfloat16)
            if width > full * LANES:
                xt[:, :, j * LANES:j * LANES + width - full * LANES] = pv[:, :, full * LANES:]

    got = hist.at[pl.ds(0, n - 1)]
    pltpu.make_async_copy(got, got, hist_r).wait()
    pltpu.make_async_copy(got, got, hist_s).wait()
    lower = jnp.zeros((2 * pos, LANES), jnp.int32)
    lower = lax.fori_loop(0, n, lambda j, a: a + jnp.where(j < me, hist[j], 0), lower)
    lane4 = lane8[:pos]
    pref[0] = jnp.zeros_like(pref[0])
    for k in range(rows):
        text = sown[k]
        limit = counts[text] - (k - start[text])
        ok = jnp.where((lane8 == text) & (lower < limit), clip_bound, 0.0)
        bnd[k] = jnp.broadcast_to(jnp.max(ok, axis=1, keepdims=True), (2 * pos, LANES))

    def partial_sums(j, store):
        base = first_tile(j) * LANES
        for t in range(texts):
            here[t] = pubs[j, t].astype(f32)
        acc = [jnp.zeros((2 * pos, LANES), f32)] * pairs
        for k in range(rows):
            row = order[k]
            text = sown[k]
            b = bnd[k]
            for c in range(pairs):
                low = pv[row, :, pl.ds(pl.multiple_of(base + c * LANES, LANES), LANES)]
                if c < pairs - 1:
                    high = pv[row, :, pl.ds(pl.multiple_of(base + hl + c * LANES, LANES), LANES)]
                else:
                    high = xt[row, :, pl.ds(pl.multiple_of(j * LANES, LANES), LANES)]
                p = jnp.concatenate([low.astype(f32), high.astype(f32)], axis=0)
                u = here[text, :, c * LANES:(c + 1) * LANES]
                acc[c] = acc[c] + jnp.minimum(jnp.maximum(p - u, -b), b)
                pref[k + 1, :, c * LANES:(c + 1) * LANES] = acc[c]
        for t in range(texts):
            store(t, pref[start[t + 1]] - pref[start[t]])

    def coded(v, scale):
        return jnp.round(v * scale).astype(jnp.int32).astype(jnp.int16)

    def decoded(q, scale):
        return q.astype(jnp.int32).astype(f32) * (1.0 / scale)

    nearer = jnp.minimum(z, half - 1 - z)

    def column(i):
        side = jnp.where(lax.rem(i, 2) == 1, -lax.div(i + 1, 2), lax.div(i, 2))
        rest = jnp.where(z < half - 1 - z, i, half - 1 - i)
        return jnp.where(i <= 2 * nearer, z + side, rest)

    def own_column(i):
        zi = column(i)

        def store(t, v):
            keep[zi, t] = v

        partial_sums(2 * zi + x, store)

    def take_turned(i):
        zi = column(i)
        part = turning(2 * zi + 1 - x)
        remote(part, part, agb_up.at[zi], agb_r.at[zi], {"ref": partner}).wait_recv()
        pass_turned(zi)

    def arrive(i, c):
        zi = column(i)
        j = 2 * zi + x
        to_partner(whole, j, zi).wait_recv()
        to_partner(straight, j, zi).start()
        along(whole, j, zi, ag_up, ag_dn, ag_r.at[j])

        @pl.when(i >= 2)
        def _():
            own_column(i - 1)
            take_turned(i - 1)

        return c

    def other_column(i, c):
        zi = column(lax.rem(i, half))
        j = 2 * zi + 1 - x

        @pl.when(i < half)
        def _():
            to_partner(straight, j, zi).wait_recv()

        def store(t, v):
            snd1[zi, t] = coded(v[:, hb:], scale1)
            sndb[zi, t] = coded(v[:, :hb], scale1)
            rowb[t] = v[:, :hb]

        partial_sums(j, store)
        remote(snd1.at[zi], rs1.at[zi], rs1_s.at[zi], rs1_r.at[zi], {"ref": partner}).start()

        @pl.when(i < half)
        def _():
            remote(sndb.at[zi], rsb.at[z], rsb_s.at[zi], rsb_r.at[z], {"ref": 2 * zi + x}).start()

        return c

    def add_partner(i, c):
        zi = column(lax.rem(i, half))
        remote(snd1.at[zi], rs1.at[zi], rs1_s.at[zi], rs1_r.at[zi], {"ref": partner}).wait_recv()
        for t in range(texts):
            keep[zi, t, :, hb:] = keep[zi, t, :, hb:] + decoded(rs1[zi, t], scale1)

        @pl.when(i < half)
        def _():
            for t in range(texts):
                snd2[zi, t] = coded(keep[zi, t], scale2)
            remote(snd2.at[zi], rs2.at[z], rs2_s.at[zi], rs2_r.at[z], {"ref": 2 * zi + x}).start()

        return c

    def add_turned(k, c):
        zi = lax.rem(z + k, half)
        remote(sndb.at[zi], rsb.at[zi], rsb_s.at[zi], rsb_r.at[zi], {"ref": 2 * zi + x}).wait_recv()
        for t in range(texts):
            rowb[t] = rowb[t] + decoded(rsb[zi, t], scale1)
        return c

    def gather(k, c):
        zi = lax.rem(z + k, half)
        remote(snd2.at[zi], rs2.at[zi], rs2_s.at[zi], rs2_r.at[zi], {"ref": 2 * zi + x}).wait_recv()
        for t in range(texts):
            keep[z, t] = keep[z, t] + decoded(rs2[zi, t], scale2)
        return c

    own_column(jnp.int32(0))
    to_partner(whole, 2 * z + 1 - x, z).wait_recv()
    pass_turned(z)
    lax.fori_loop(1, half, arrive, 0)
    take_turned(jnp.int32(half - 1))
    lax.fori_loop(1, half + 1, other_column, 0)
    own_column(jnp.int32(half - 1))
    lax.fori_loop(1, half + 1, add_partner, 0)
    lax.fori_loop(1, half, add_turned, 0)
    for t in range(texts):
        sndf[t] = coded(rowb[t], scale3)
    last = remote(sndf, rsf, rsf_s, rsf_r, {"ref": partner})
    last.start()
    lax.fori_loop(1, half, gather, 0)
    last.wait_recv()
    for t in range(texts):
        keep[z, t, :, :hb] = keep[z, t, :, :hb] + decoded(rsf[t], scale3)

    first_column = (mv * n + me) * piece
    at_column = lax.broadcasted_iota(jnp.int32, (pos, piece), 1) + first_column
    at_pos = lax.broadcasted_iota(jnp.int32, (pos, 1), 0)
    lse_all = jnp.zeros((pos, LANES), f32)
    picked_all = jnp.zeros((pos, LANES), f32)
    for t in range(texts):
        both = keep[z, t]
        summed = jnp.concatenate([both[:pos], both[pos:]], axis=1)
        summed = pltpu.roll(summed, lax.rem(wl - shift, wl), 1)[:, :piece]
        root = jnp.sqrt(jnp.full((pos, LANES), counts[t].astype(f32), f32))
        factor = (1.0 / (clip_bound * root))[:, :1]
        combined = pub[t].astype(f32) + summed * factor + noise[t].astype(f32)
        combined_out[t] = combined
        peak = jnp.max(combined, axis=1, keepdims=True)
        total = jnp.sum(jnp.exp(combined - peak), axis=1, keepdims=True)
        token = jnp.zeros((pos, 1), jnp.int32)
        for p in range(pos):
            token = jnp.where(at_pos == p, tokens[t, p], token)
        picked = jnp.sum(jnp.where(at_column == token, combined, 0.0), axis=1, keepdims=True)
        lse_all = jnp.where(lane4 == t, peak + jnp.log(total), lse_all)
        picked_all = jnp.where(lane4 == t, picked, picked_all)

    def exchange(slots, send, recv, index, count, axis, lse, picked):
        slots[index, :pos] = lse
        slots[index, pos:2 * pos] = picked

        def send_one(k, c):
            remote(slots.at[index], slots.at[index], send, recv, {axis: lax.rem(index + k, count)}).start()
            return c

        lax.fori_loop(1, count, send_one, 0)
        others = slots.at[pl.ds(0, count - 1)]
        pltpu.make_async_copy(others, others, recv).wait()
        pltpu.make_async_copy(others, others, send).wait()
        top = lax.fori_loop(1, count, lambda j, a: jnp.maximum(a, slots[j, :pos]), slots[0, :pos])
        zero = jnp.zeros((pos, LANES), f32)
        total, found = lax.fori_loop(
            0, count,
            lambda j, a: (a[0] + jnp.exp(slots[j, :pos] - top), a[1] + slots[j, pos:2 * pos]),
            (zero, zero),
        )
        return top + jnp.log(total), found

    lse, picked = exchange(st1, st1_s, st1_r, mv, nv, "voc", lse_all, picked_all)
    lse, picked = exchange(st2, st2_s, st2_r, me, n, "ref", lse, picked)
    stats_out[0] = lse
    stats_out[1] = picked

    def left(src, sem):
        remote(src, src, sem, ag_r.at[me], {"ref": partner}).wait_send()

    def sent(i, c):
        left(snd1.at[i], rs1_s.at[i])

        @pl.when((i <= z) & (z < half - 1))
        def _():
            left(whole(me), ag_up.at[i])
            left(turning(me), agb_up.at[i])

        @pl.when((i >= z) & (z > 0))
        def _():
            left(whole(me), ag_dn.at[i])
            left(turning(me), agb_dn.at[i])

        @pl.when(i != z)
        def _():
            left(straight(me), ag_x.at[i])
            left(snd2.at[i], rs2_s.at[i])
            left(sndb.at[i], rsb_s.at[i])

        return c

    left(whole(me), ag_x.at[z])
    left(sndf, rsf_s)
    lax.fori_loop(0, half, sent, 0)


def finish(texts, pos, combined, stats, logprobs, target):
    lse = stats[0]
    score = stats[1] - lse
    at_pos = lax.broadcasted_iota(jnp.int32, (pos, pos), 0)
    at_lane = lax.broadcasted_iota(jnp.int32, (pos, pos), 1)
    for t in range(texts):
        logprobs[t] = combined[t] - lse[:, t:t + 1]
        column = jnp.where(at_pos == at_lane, score[:, t:t + 1], 0.0)
        target[t:t + 1, :] = jnp.sum(column, axis=0, keepdims=True)


def body(n, nv, private_logits, public_logits, noise, owner, counts, tokens):
    rows, pos, width = private_logits.shape
    texts, _, piece = public_logits.shape
    half = n // 2
    full = width // LANES
    win = max(-(-((j * piece) % LANES + piece) // LANES) for j in range(n))
    while min(j * piece - LANES * min(j * piece // LANES, full + 1 - win) for j in range(n)) < 0:
        win += 1
    win += win % 2
    wl = win * LANES
    hl = wl // 2
    hb = turned(win // 2) * LANES
    bf16, f32, i16 = jnp.bfloat16, jnp.float32, jnp.int16
    smem = pl.BlockSpec(memory_space=pltpu.SMEM)
    vmem = pl.BlockSpec(memory_space=pltpu.VMEM)
    dma = pltpu.SemaphoreType.DMA
    combined, stats = pl.pallas_call(
        functools.partial(kernel, n, nv, rows, texts, pos, width, piece, win),
        out_shape=(
            jax.ShapeDtypeStruct((texts, pos, piece), f32),
            jax.ShapeDtypeStruct((2, pos, LANES), f32),
        ),
        in_specs=[smem, smem, smem, pl.BlockSpec(memory_space=pl.ANY), vmem, vmem],
        out_specs=(vmem, vmem),
        scratch_shapes=[
            pltpu.VMEM((rows, pos, width), bf16),
            pltpu.VMEM((rows, pos, n * LANES), bf16),
            pltpu.VMEM((texts, pos, wl), f32),
            pltpu.VMEM((n, texts, 2 * pos, hl), bf16),
            pltpu.VMEM((texts, 2 * pos, hl), f32),
            pltpu.VMEM((rows + 1, 2 * pos, hl), f32),
            pltpu.VMEM((half, texts, 2 * pos, hl), f32),
            pltpu.VMEM((half, texts, 2 * pos, hl - hb), i16),
            pltpu.VMEM((half, texts, 2 * pos, hl - hb), i16),
            pltpu.VMEM((half, texts, 2 * pos, hl), i16),
            pltpu.VMEM((half, texts, 2 * pos, hl), i16),
            pltpu.VMEM((texts, 2 * pos, hb), f32),
            pltpu.VMEM((half, texts, 2 * pos, hb), i16),
            pltpu.VMEM((half, texts, 2 * pos, hb), i16),
            pltpu.VMEM((texts, 2 * pos, hb), i16),
            pltpu.VMEM((texts, 2 * pos, hb), i16),
            pltpu.VMEM((n, 2 * pos, LANES), jnp.int32),
            pltpu.VMEM((nv, 2 * pos, LANES), f32),
            pltpu.VMEM((n, 2 * pos, LANES), f32),
            pltpu.VMEM((rows, 2 * pos, LANES), f32),
            pltpu.SMEM((rows,), jnp.int32),
            pltpu.SMEM((rows,), jnp.int32),
            pltpu.SMEM((texts + 1,), jnp.int32),
            dma, dma, dma,
            dma((half,)), dma((half,)), dma((half,)), dma((n,)),
            dma((half,)), dma((half,)), dma((half,)),
            dma((half,)), dma((half,)), dma((half,)), dma((half,)),
            dma((half,)), dma((half,)), dma, dma,
            dma, dma, dma, dma,
        ],
        compiler_params=pltpu.CompilerParams(
            collective_id=0, has_side_effects=True, vmem_limit_bytes=56 * 1024 * 1024
        ),
        cost_estimate=pl.CostEstimate(
            flops=6 * rows * pos * width, bytes_accessed=2 * rows * pos * width, transcendentals=0
        ),
        name="private_scores",
    )(owner, counts, tokens, private_logits, public_logits, noise)
    return pl.pallas_call(
        functools.partial(finish, texts, pos),
        out_shape=(
            jax.ShapeDtypeStruct((texts, pos, piece), f32),
            jax.ShapeDtypeStruct((texts, pos), f32),
        ),
        in_specs=[vmem, vmem],
        out_specs=(vmem, vmem),
        name="subtract_lse",
    )(combined, stats)


def solution(mesh):
    return jax.shard_map(
        functools.partial(body, mesh.shape["ref"], mesh.shape["voc"]),
        mesh=mesh,
        in_specs=(
            P("ref", None, "voc"),
            P(None, None, ("voc", "ref")),
            P(None, None, ("voc", "ref")),
            P("ref"),
            P(),
            P(),
        ),
        out_specs=(P(None, None, ("voc", "ref")), P()),
        check_vma=False,
    )
```

```python
import functools

import jax
import jax.numpy as jnp
from jax import lax
from jax.experimental import pallas as pl
from jax.experimental.pallas import tpu as pltpu
from jax.sharding import PartitionSpec as P

clip_bound = 2.0
LANES = 128
MESH = pl.DeviceIdType.MESH


def fixed_point(rows):
    scale = 1
    while scale * 2 * clip_bound * rows <= 32000:
        scale *= 2
    return float(scale)


def turned(pairs):
    return (pairs + 3) // 6


def kernel(
    n, nv, rows, texts, pos, width, piece, win,
    owner, counts, tokens, priv, pub, noise,
    combined_hbm, stats_out,
    combined_out,    pv, xt, pubf, pubs, here, pref, keep, snd1, rs1, snd2, rs2, rowb, sndb, rsb, sndf, rsf,
    hist, st1, st2, bnd, order, sown, start,
    priv_sem, hist_s, hist_r, ag_x, ag_up, ag_dn, ag_r, agb_up, agb_dn, agb_r,
    rs1_s, rs1_r, rs2_s, rs2_r, rsb_s, rsb_r, rsf_s, rsf_r,
    st1_s, st1_r, st2_s, st2_r, out_sem,
):
    f32 = jnp.float32
    half = n // 2
    full = width // LANES
    wl = win * LANES
    pairs = win // 2
    hl = pairs * LANES
    hb = turned(pairs) * LANES
    me = lax.axis_index("ref")
    mv = lax.axis_index("voc")
    z = lax.div(me, 2)
    x = lax.rem(me, 2)
    partner = me + 1 - 2 * x
    scale1 = fixed_point(rows)
    scale2 = fixed_point(min(2 * rows, n * rows // texts))
    scale3 = fixed_point(min(half * rows, n * rows // texts))

    def first_tile(j):
        return jnp.minimum(lax.div(j * piece, LANES), full + 1 - win)

    def remote(src, dst, send, recv, peer):
        return pltpu.make_async_remote_copy(
            src_ref=src, dst_ref=dst, send_sem=send, recv_sem=recv,
            device_id=peer, device_id_type=MESH,
        )

    load = pltpu.make_async_copy(priv, pv, priv_sem)
    load.start()
    barrier = pltpu.get_barrier_semaphore()

    def greet(k, c):
        pl.semaphore_signal(barrier, inc=1, device_id={"ref": lax.rem(me + k, n)}, device_id_type=MESH)
        return c

    def greet_voc(k, c):
        pl.semaphore_signal(barrier, inc=1, device_id={"voc": lax.rem(mv + k, nv)}, device_id_type=MESH)
        return c

    lax.fori_loop(1, n, greet, 0)
    lax.fori_loop(1, nv, greet_voc, 0)

    shift = me * piece - first_tile(me) * LANES
    pubf[...] = jnp.zeros_like(pubf)
    for t in range(texts):
        pubf[t, :, :piece] = pub[t].astype(f32)
    for t in range(texts):
        moved = pltpu.roll(pubf[t], shift, 1)
        pubs[me, t] = jnp.concatenate([moved[:, :hl], moved[:, hl:]], axis=0).astype(jnp.bfloat16)

    own = [owner[r] for r in range(rows)]
    hits = [sum((o == t).astype(jnp.int32) for o in own) for t in range(texts)]
    lane8 = lax.broadcasted_iota(jnp.int32, (2 * pos, LANES), 1)
    mine = jnp.zeros((2 * pos, LANES), jnp.int32)
    for t in range(texts):
        mine = jnp.where(lane8 == t, hits[t], mine)
    hist[me] = mine

    pl.semaphore_wait(barrier, n - 1 + nv - 1)

    def whole(j):
        return pubs.at[j]

    def straight(j):
        return pubs.at[j, :, :, pl.ds(hb, hl - hb)]

    def turning(j):
        return pubs.at[j, :, :, pl.ds(0, hb)]

    def to_partner(part, j, zi):
        return remote(part(j), part(j), ag_x.at[zi], ag_r.at[j], {"ref": partner})

    def along(part, j, zi, up, down, recv):
        @pl.when((zi <= z) & (z < half - 1))
        def _():
            remote(part(j), part(j), up.at[zi], recv, {"ref": me + 2}).start()

        @pl.when((zi >= z) & (z > 0))
        def _():
            remote(part(j), part(j), down.at[zi], recv, {"ref": me - 2}).start()

    def pass_turned(zi):
        j = 2 * zi + 1 - x
        along(turning, j, zi, agb_up, agb_dn, agb_r.at[zi])

    def send_hist(k, c):
        remote(hist.at[me], hist.at[me], hist_s, hist_r, {"ref": lax.rem(me + k, n)}).start()
        return c

    lax.fori_loop(1, n, send_hist, 0)
    to_partner(whole, me, z).start()
    along(whole, me, z, ag_up, ag_dn, ag_r.at[me])

    begin = [jnp.int32(0)]
    for t in range(texts):
        begin.append(begin[-1] + hits[t])
    for t in range(texts + 1):
        start[t] = begin[t]
    place = []
    for r in range(rows):
        before = jnp.int32(0)
        for q in range(rows):
            if q < r:
                before = before + (own[q] <= own[r]).astype(jnp.int32)
            elif q > r:
                before = before + (own[q] < own[r]).astype(jnp.int32)
        place.append(before)
    for k in range(rows):
        at = jnp.int32(0)
        for r in range(rows):
            at = at + jnp.where(place[r] == k, r, 0)
        order[k] = at
        sown[k] = sum((begin[t] <= k).astype(jnp.int32) for t in range(1, texts))

    load.wait()
    for j in range(n):
        s = min(j * piece // LANES, full + 1 - win) + win - 1
        if s < full:
            xt[:, :, j * LANES:(j + 1) * LANES] = pv[:, :, s * LANES:(s + 1) * LANES]
        else:
            xt[:, :, j * LANES:(j + 1) * LANES] = jnp.zeros((rows, pos, LANES), jnp.bfloat16)
            if width > full * LANES:
                xt[:, :, j * LANES:j * LANES + width - full * LANES] = pv[:, :, full * LANES:]

    got = hist.at[pl.ds(0, n - 1)]
    pltpu.make_async_copy(got, got, hist_r).wait()
    pltpu.make_async_copy(got, got, hist_s).wait()
    lower = jnp.zeros((2 * pos, LANES), jnp.int32)
    lower = lax.fori_loop(0, n, lambda j, a: a + jnp.where(j < me, hist[j], 0), lower)
    lane4 = lane8[:pos]
    pref[0] = jnp.zeros_like(pref[0])
    for k in range(rows):
        text = sown[k]
        limit = counts[text] - (k - start[text])
        ok = jnp.where((lane8 == text) & (lower < limit), clip_bound, 0.0)
        bnd[k] = jnp.broadcast_to(jnp.max(ok, axis=1, keepdims=True), (2 * pos, LANES))

    def partial_sums(j, store):
        base = first_tile(j) * LANES
        for t in range(texts):
            here[t] = pubs[j, t].astype(f32)
        acc = [jnp.zeros((2 * pos, LANES), f32)] * pairs
        for k in range(rows):
            row = order[k]
            text = sown[k]
            b = bnd[k]
            for c in range(pairs):
                low = pv[row, :, pl.ds(pl.multiple_of(base + c * LANES, LANES), LANES)]
                if c < pairs - 1:
                    high = pv[row, :, pl.ds(pl.multiple_of(base + hl + c * LANES, LANES), LANES)]
                else:
                    high = xt[row, :, pl.ds(pl.multiple_of(j * LANES, LANES), LANES)]
                p = jnp.concatenate([low.astype(f32), high.astype(f32)], axis=0)
                u = here[text, :, c * LANES:(c + 1) * LANES]
                acc[c] = acc[c] + jnp.minimum(jnp.maximum(p - u, -b), b)
                pref[k + 1, :, c * LANES:(c + 1) * LANES] = acc[c]
        for t in range(texts):
            store(t, pref[start[t + 1]] - pref[start[t]])

    def coded(v, scale):
        return jnp.round(v * scale).astype(jnp.int32).astype(jnp.int16)

    def decoded(q, scale):
        return q.astype(jnp.int32).astype(f32) * (1.0 / scale)

    nearer = jnp.minimum(z, half - 1 - z)

    def column(i):
        side = jnp.where(lax.rem(i, 2) == 1, -lax.div(i + 1, 2), lax.div(i, 2))
        rest = jnp.where(z < half - 1 - z, i, half - 1 - i)
        return jnp.where(i <= 2 * nearer, z + side, rest)

    def own_column(i):
        zi = column(i)

        def store(t, v):
            keep[zi, t] = v

        partial_sums(2 * zi + x, store)

    def take_turned(i):
        zi = column(i)
        part = turning(2 * zi + 1 - x)
        remote(part, part, agb_up.at[zi], agb_r.at[zi], {"ref": partner}).wait_recv()
        pass_turned(zi)

    def other_column(i, c):
        zi = column(lax.rem(i, half))
        j = 2 * zi + 1 - x

        @pl.when(i < half)
        def _():
            to_partner(straight, j, zi).wait_recv()

        def store(t, v):
            snd1[zi, t] = coded(v[:, hb:], scale1)
            sndb[zi, t] = coded(v[:, :hb], scale1)
            rowb[t] = v[:, :hb]

        partial_sums(j, store)
        remote(snd1.at[zi], rs1.at[zi], rs1_s.at[zi], rs1_r.at[zi], {"ref": partner}).start()

        @pl.when(i < half)
        def _():
            remote(sndb.at[zi], rsb.at[z], rsb_s.at[zi], rsb_r.at[z], {"ref": 2 * zi + x}).start()

        return c

    def arrive(i, c):
        zi = column(i)
        j = 2 * zi + x
        to_partner(whole, j, zi).wait_recv()
        to_partner(straight, j, zi).start()
        along(whole, j, zi, ag_up, ag_dn, ag_r.at[j])

        @pl.when(i >= 2)
        def _():
            take_turned(i - 1)
            other_column(i - 1, 0)

        return c

    def add_partner(i, c):
        zi = column(lax.rem(i, half))

        @pl.when(i < half)
        def _():
            own_column(i)

        remote(snd1.at[zi], rs1.at[zi], rs1_s.at[zi], rs1_r.at[zi], {"ref": partner}).wait_recv()
        for t in range(texts):
            keep[zi, t, :, hb:] = keep[zi, t, :, hb:] + decoded(rs1[zi, t], scale1)

        @pl.when(i < half)
        def _():
            for t in range(texts):
                snd2[zi, t] = coded(keep[zi, t], scale2)
            remote(snd2.at[zi], rs2.at[z], rs2_s.at[zi], rs2_r.at[z], {"ref": 2 * zi + x}).start()

        return c

    def add_turned(k, c):
        zi = lax.rem(z + k, half)
        remote(sndb.at[zi], rsb.at[zi], rsb_s.at[zi], rsb_r.at[zi], {"ref": 2 * zi + x}).wait_recv()
        for t in range(texts):
            rowb[t] = rowb[t] + decoded(rsb[zi, t], scale1)
        return c

    def gather(k, c):
        zi = lax.rem(z + k, half)
        remote(snd2.at[zi], rs2.at[zi], rs2_s.at[zi], rs2_r.at[zi], {"ref": 2 * zi + x}).wait_recv()
        for t in range(texts):
            keep[z, t] = keep[z, t] + decoded(rs2[zi, t], scale2)
        return c

    own_column(jnp.int32(0))
    to_partner(whole, 2 * z + 1 - x, z).wait_recv()
    pass_turned(z)
    lax.fori_loop(1, half, arrive, 0)
    take_turned(jnp.int32(half - 1))
    lax.fori_loop(half - 1, half + 1, other_column, 0)
    lax.fori_loop(1, half + 1, add_partner, 0)
    lax.fori_loop(1, half, add_turned, 0)
    for t in range(texts):
        sndf[t] = coded(rowb[t], scale3)
    last = remote(sndf, rsf, rsf_s, rsf_r, {"ref": partner})
    last.start()
    lax.fori_loop(1, half, gather, 0)
    last.wait_recv()
    for t in range(texts):
        keep[z, t, :, :hb] = keep[z, t, :, :hb] + decoded(rsf[t], scale3)

    first_column = (mv * n + me) * piece
    at_column = lax.broadcasted_iota(jnp.int32, (pos, piece), 1) + first_column
    at_pos = lax.broadcasted_iota(jnp.int32, (pos, 1), 0)
    lse_all = jnp.zeros((pos, LANES), f32)
    picked_all = jnp.zeros((pos, LANES), f32)
    for t in range(texts):
        both = keep[z, t]
        summed = jnp.concatenate([both[:pos], both[pos:]], axis=1)
        summed = pltpu.roll(summed, lax.rem(wl - shift, wl), 1)[:, :piece]
        root = jnp.sqrt(jnp.full((pos, LANES), counts[t].astype(f32), f32))
        factor = (1.0 / (clip_bound * root))[:, :1]
        combined = pub[t].astype(f32) + summed * factor + noise[t].astype(f32)
        combined_out[t] = combined
        peak = jnp.max(combined, axis=1, keepdims=True)
        total = jnp.sum(jnp.exp(combined - peak), axis=1, keepdims=True)
        token = jnp.zeros((pos, 1), jnp.int32)
        for p in range(pos):
            token = jnp.where(at_pos == p, tokens[t, p], token)
        picked = jnp.sum(jnp.where(at_column == token, combined, 0.0), axis=1, keepdims=True)
        lse_all = jnp.where(lane4 == t, peak + jnp.log(total), lse_all)
        picked_all = jnp.where(lane4 == t, picked, picked_all)

    out = pltpu.make_async_copy(combined_out, combined_hbm, out_sem)
    out.start()

    def exchange(slots, send, recv, index, count, axis, lse, picked):
        slots[index, :pos] = lse
        slots[index, pos:2 * pos] = picked

        def send_one(k, c):
            remote(slots.at[index], slots.at[index], send, recv, {axis: lax.rem(index + k, count)}).start()
            return c

        lax.fori_loop(1, count, send_one, 0)
        others = slots.at[pl.ds(0, count - 1)]
        pltpu.make_async_copy(others, others, recv).wait()
        pltpu.make_async_copy(others, others, send).wait()
        top = lax.fori_loop(1, count, lambda j, a: jnp.maximum(a, slots[j, :pos]), slots[0, :pos])
        zero = jnp.zeros((pos, LANES), f32)
        total, found = lax.fori_loop(
            0, count,
            lambda j, a: (a[0] + jnp.exp(slots[j, :pos] - top), a[1] + slots[j, pos:2 * pos]),
            (zero, zero),
        )
        return top + jnp.log(total), found

    lse, picked = exchange(st1, st1_s, st1_r, mv, nv, "voc", lse_all, picked_all)
    lse, picked = exchange(st2, st2_s, st2_r, me, n, "ref", lse, picked)
    stats_out[0] = lse
    stats_out[1] = picked
    out.wait()

    def left(src, sem):
        remote(src, src, sem, ag_r.at[me], {"ref": partner}).wait_send()

    def sent(i, c):
        left(snd1.at[i], rs1_s.at[i])

        @pl.when((i <= z) & (z < half - 1))
        def _():
            left(whole(me), ag_up.at[i])
            left(turning(me), agb_up.at[i])

        @pl.when((i >= z) & (z > 0))
        def _():
            left(whole(me), ag_dn.at[i])
            left(turning(me), agb_dn.at[i])

        @pl.when(i != z)
        def _():
            left(straight(me), ag_x.at[i])
            left(snd2.at[i], rs2_s.at[i])
            left(sndb.at[i], rsb_s.at[i])

        return c

    left(whole(me), ag_x.at[z])
    left(sndf, rsf_s)
    lax.fori_loop(0, half, sent, 0)


def finish(texts, pos, combined, stats, logprobs, target):
    lse = stats[0]
    score = stats[1] - lse
    at_pos = lax.broadcasted_iota(jnp.int32, (pos, pos), 0)
    at_lane = lax.broadcasted_iota(jnp.int32, (pos, pos), 1)
    for t in range(texts):
        logprobs[t] = combined[t] - lse[:, t:t + 1]
        column = jnp.where(at_pos == at_lane, score[:, t:t + 1], 0.0)
        target[t:t + 1, :] = jnp.sum(column, axis=0, keepdims=True)


def body(n, nv, private_logits, public_logits, noise, owner, counts, tokens):
    rows, pos, width = private_logits.shape
    texts, _, piece = public_logits.shape
    half = n // 2
    full = width // LANES
    win = max(-(-((j * piece) % LANES + piece) // LANES) for j in range(n))
    while min(j * piece - LANES * min(j * piece // LANES, full + 1 - win) for j in range(n)) < 0:
        win += 1
    win += win % 2
    wl = win * LANES
    hl = wl // 2
    hb = turned(win // 2) * LANES
    bf16, f32, i16 = jnp.bfloat16, jnp.float32, jnp.int16
    smem = pl.BlockSpec(memory_space=pltpu.SMEM)
    vmem = pl.BlockSpec(memory_space=pltpu.VMEM)
    dma = pltpu.SemaphoreType.DMA
    combined, stats = pl.pallas_call(
        functools.partial(kernel, n, nv, rows, texts, pos, width, piece, win),
        out_shape=(
            jax.ShapeDtypeStruct((texts, pos, piece), f32),
            jax.ShapeDtypeStruct((2, pos, LANES), f32),
        ),
        in_specs=[smem, smem, smem, pl.BlockSpec(memory_space=pl.ANY), vmem, vmem],
        out_specs=(pl.BlockSpec(memory_space=pl.ANY), vmem),
        scratch_shapes=[
            pltpu.VMEM((texts, pos, piece), f32),
            pltpu.VMEM((rows, pos, width), bf16),
            pltpu.VMEM((rows, pos, n * LANES), bf16),
            pltpu.VMEM((texts, pos, wl), f32),
            pltpu.VMEM((n, texts, 2 * pos, hl), bf16),
            pltpu.VMEM((texts, 2 * pos, hl), f32),
            pltpu.VMEM((rows + 1, 2 * pos, hl), f32),
            pltpu.VMEM((half, texts, 2 * pos, hl), f32),
            pltpu.VMEM((half, texts, 2 * pos, hl - hb), i16),
            pltpu.VMEM((half, texts, 2 * pos, hl - hb), i16),
            pltpu.VMEM((half, texts, 2 * pos, hl), i16),
            pltpu.VMEM((half, texts, 2 * pos, hl), i16),
            pltpu.VMEM((texts, 2 * pos, hb), f32),
            pltpu.VMEM((half, texts, 2 * pos, hb), i16),
            pltpu.VMEM((half, texts, 2 * pos, hb), i16),
            pltpu.VMEM((texts, 2 * pos, hb), i16),
            pltpu.VMEM((texts, 2 * pos, hb), i16),
            pltpu.VMEM((n, 2 * pos, LANES), jnp.int32),
            pltpu.VMEM((nv, 2 * pos, LANES), f32),
            pltpu.VMEM((n, 2 * pos, LANES), f32),
            pltpu.VMEM((rows, 2 * pos, LANES), f32),
            pltpu.SMEM((rows,), jnp.int32),
            pltpu.SMEM((rows,), jnp.int32),
            pltpu.SMEM((texts + 1,), jnp.int32),
            dma, dma, dma,
            dma((half,)), dma((half,)), dma((half,)), dma((n,)),
            dma((half,)), dma((half,)), dma((half,)),
            dma((half,)), dma((half,)), dma((half,)), dma((half,)),
            dma((half,)), dma((half,)), dma, dma,
            dma, dma, dma, dma, dma,
        ],
        compiler_params=pltpu.CompilerParams(
            collective_id=0, has_side_effects=True, vmem_limit_bytes=56 * 1024 * 1024
        ),
        cost_estimate=pl.CostEstimate(
            flops=6 * rows * pos * width, bytes_accessed=2 * rows * pos * width, transcendentals=0
        ),
        name="private_scores",
    )(owner, counts, tokens, private_logits, public_logits, noise)
    return pl.pallas_call(
        functools.partial(finish, texts, pos),
        out_shape=(
            jax.ShapeDtypeStruct((texts, pos, piece), f32),
            jax.ShapeDtypeStruct((texts, pos), f32),
        ),
        in_specs=[vmem, vmem],
        out_specs=(vmem, vmem),
        name="subtract_lse",
    )(combined, stats)


def solution(mesh):
    return jax.shard_map(
        functools.partial(body, mesh.shape["ref"], mesh.shape["voc"]),
        mesh=mesh,
        in_specs=(
            P("ref", None, "voc"),
            P(None, None, ("voc", "ref")),
            P(None, None, ("voc", "ref")),
            P("ref"),
            P(),
            P(),
        ),
        out_specs=(P(None, None, ("voc", "ref")), P()),
        check_vma=False,
    )
```

```python
import functools

import jax
import jax.numpy as jnp
from jax import lax
from jax.experimental import pallas as pl
from jax.experimental.pallas import tpu as pltpu
from jax.sharding import PartitionSpec as P

clip_bound = 2.0
LANES = 128
MESH = pl.DeviceIdType.MESH


def fixed_point(rows):
    scale = 1
    while scale * 2 * clip_bound * rows <= 32000:
        scale *= 2
    return float(scale)


def turned(pairs):
    return (pairs + 3) // 6


def kernel(
    n, nv, rows, texts, pos, width, piece, win,
    owner, counts, tokens, priv, pub, noise,
    combined_hbm, stats_out,
    combined_out,    pv, xt, pubf, pubs, here, pref, keep, snd1, rs1, snd2, rs2, rowb, sndb, rsb, sndf, rsf,
    hist, st1, st2, bnd, order, sown, start,
    priv_sem, hist_s, hist_r, ag_x, ag_up, ag_dn, ag_r, agb_up, agb_dn, agb_r,
    rs1_s, rs1_r, rs2_s, rs2_r, rsb_s, rsb_r, rsf_s, rsf_r,
    st1_s, st1_r, st2_s, st2_r, out_sem,
):
    f32 = jnp.float32
    half = n // 2
    full = width // LANES
    wl = win * LANES
    pairs = win // 2
    hl = pairs * LANES
    hb = turned(pairs) * LANES
    me = lax.axis_index("ref")
    mv = lax.axis_index("voc")
    z = lax.div(me, 2)
    x = lax.rem(me, 2)
    partner = me + 1 - 2 * x
    scale1 = fixed_point(rows)
    scale2 = fixed_point(min(2 * rows, n * rows // texts))
    scale3 = fixed_point(min(half * rows, n * rows // texts))

    def first_tile(j):
        return jnp.minimum(lax.div(j * piece, LANES), full + 1 - win)

    def remote(src, dst, send, recv, peer):
        return pltpu.make_async_remote_copy(
            src_ref=src, dst_ref=dst, send_sem=send, recv_sem=recv,
            device_id=peer, device_id_type=MESH,
        )

    load = pltpu.make_async_copy(priv, pv, priv_sem)
    load.start()
    barrier = pltpu.get_barrier_semaphore()

    def greet(k, c):
        pl.semaphore_signal(barrier, inc=1, device_id={"ref": lax.rem(me + k, n)}, device_id_type=MESH)
        return c

    def greet_voc(k, c):
        pl.semaphore_signal(barrier, inc=1, device_id={"voc": lax.rem(mv + k, nv)}, device_id_type=MESH)
        return c

    lax.fori_loop(1, n, greet, 0)
    lax.fori_loop(1, nv, greet_voc, 0)

    shift = me * piece - first_tile(me) * LANES
    pubf[...] = jnp.zeros_like(pubf)
    for t in range(texts):
        pubf[t, :, :piece] = pub[t].astype(f32)
    for t in range(texts):
        moved = pltpu.roll(pubf[t], shift, 1)
        pubs[me, t] = jnp.concatenate([moved[:, :hl], moved[:, hl:]], axis=0).astype(jnp.bfloat16)

    own = [owner[r] for r in range(rows)]
    hits = [sum((o == t).astype(jnp.int32) for o in own) for t in range(texts)]
    lane8 = lax.broadcasted_iota(jnp.int32, (2 * pos, LANES), 1)
    mine = jnp.zeros((2 * pos, LANES), jnp.int32)
    for t in range(texts):
        mine = jnp.where(lane8 == t, hits[t], mine)
    hist[me] = mine

    pl.semaphore_wait(barrier, n - 1 + nv - 1)

    def whole(j):
        return pubs.at[j]

    def straight(j):
        return pubs.at[j, :, :, pl.ds(hb, hl - hb)]

    def turning(j):
        return pubs.at[j, :, :, pl.ds(0, hb)]

    def to_partner(part, j, zi):
        return remote(part(j), part(j), ag_x.at[zi], ag_r.at[j], {"ref": partner})

    def along(part, j, zi, up, down, recv):
        @pl.when((zi <= z) & (z < half - 1))
        def _():
            remote(part(j), part(j), up.at[zi], recv, {"ref": me + 2}).start()

        @pl.when((zi >= z) & (z > 0))
        def _():
            remote(part(j), part(j), down.at[zi], recv, {"ref": me - 2}).start()

    def pass_turned(zi):
        j = 2 * zi + 1 - x
        along(turning, j, zi, agb_up, agb_dn, agb_r.at[zi])

    def send_hist(k, c):
        remote(hist.at[me], hist.at[me], hist_s, hist_r, {"ref": lax.rem(me + k, n)}).start()
        return c

    lax.fori_loop(1, n, send_hist, 0)
    to_partner(whole, me, z).start()
    along(whole, me, z, ag_up, ag_dn, ag_r.at[me])

    begin = [jnp.int32(0)]
    for t in range(texts):
        begin.append(begin[-1] + hits[t])
    for t in range(texts + 1):
        start[t] = begin[t]
    place = []
    for r in range(rows):
        before = jnp.int32(0)
        for q in range(rows):
            if q < r:
                before = before + (own[q] <= own[r]).astype(jnp.int32)
            elif q > r:
                before = before + (own[q] < own[r]).astype(jnp.int32)
        place.append(before)
    for k in range(rows):
        at = jnp.int32(0)
        for r in range(rows):
            at = at + jnp.where(place[r] == k, r, 0)
        order[k] = at
        sown[k] = sum((begin[t] <= k).astype(jnp.int32) for t in range(1, texts))

    load.wait()
    for j in range(n):
        s = min(j * piece // LANES, full + 1 - win) + win - 1
        if s < full:
            xt[:, :, j * LANES:(j + 1) * LANES] = pv[:, :, s * LANES:(s + 1) * LANES]
        else:
            xt[:, :, j * LANES:(j + 1) * LANES] = jnp.zeros((rows, pos, LANES), jnp.bfloat16)
            if width > full * LANES:
                xt[:, :, j * LANES:j * LANES + width - full * LANES] = pv[:, :, full * LANES:]

    got = hist.at[pl.ds(0, n - 1)]
    pltpu.make_async_copy(got, got, hist_r).wait()
    pltpu.make_async_copy(got, got, hist_s).wait()
    lower = jnp.zeros((2 * pos, LANES), jnp.int32)
    lower = lax.fori_loop(0, n, lambda j, a: a + jnp.where(j < me, hist[j], 0), lower)
    lane4 = lane8[:pos]
    pref[0] = jnp.zeros_like(pref[0])
    for k in range(rows):
        text = sown[k]
        limit = counts[text] - (k - start[text])
        ok = jnp.where((lane8 == text) & (lower < limit), clip_bound, 0.0)
        bnd[k] = jnp.broadcast_to(jnp.max(ok, axis=1, keepdims=True), (2 * pos, LANES))

    def partial_sums(j, store):
        base = first_tile(j) * LANES
        for t in range(texts):
            here[t] = pubs[j, t].astype(f32)
        base = pl.multiple_of(base, LANES)
        middle = pl.multiple_of(base + hl, LANES)
        end = pl.multiple_of(j * LANES, LANES)
        acc = jnp.zeros((2 * pos, hl), f32)
        for k in range(rows):
            row = order[k]
            b = jnp.concatenate([bnd[k]] * pairs, axis=1)
            low = pv[row, :, pl.ds(base, hl)].astype(f32)
            high = pv[row, :, pl.ds(middle, hl - LANES)].astype(f32)
            high = jnp.concatenate([high, xt[row, :, pl.ds(end, LANES)].astype(f32)], axis=1)
            p = jnp.concatenate([low, high], axis=0)
            acc = acc + jnp.minimum(jnp.maximum(p - here[sown[k]], -b), b)
            pref[k + 1] = acc
        for t in range(texts):
            store(t, pref[start[t + 1]] - pref[start[t]])

    def coded(v, scale):
        return jnp.round(v * scale).astype(jnp.int32).astype(jnp.int16)

    def decoded(q, scale):
        return q.astype(jnp.int32).astype(f32) * (1.0 / scale)

    nearer = jnp.minimum(z, half - 1 - z)

    def column(i):
        side = jnp.where(lax.rem(i, 2) == 1, -lax.div(i + 1, 2), lax.div(i, 2))
        rest = jnp.where(z < half - 1 - z, i, half - 1 - i)
        return jnp.where(i <= 2 * nearer, z + side, rest)

    def own_column(i):
        zi = column(i)

        def store(t, v):
            keep[zi, t] = v

        partial_sums(2 * zi + x, store)

    def take_turned(i):
        zi = column(i)
        part = turning(2 * zi + 1 - x)
        remote(part, part, agb_up.at[zi], agb_r.at[zi], {"ref": partner}).wait_recv()
        pass_turned(zi)

    def other_column(i, c):
        zi = column(lax.rem(i, half))
        j = 2 * zi + 1 - x

        @pl.when(i < half)
        def _():
            to_partner(straight, j, zi).wait_recv()

        def store(t, v):
            snd1[zi, t] = coded(v[:, hb:], scale1)
            sndb[zi, t] = coded(v[:, :hb], scale1)
            rowb[t] = v[:, :hb]

        partial_sums(j, store)
        remote(snd1.at[zi], rs1.at[zi], rs1_s.at[zi], rs1_r.at[zi], {"ref": partner}).start()

        @pl.when(i < half)
        def _():
            remote(sndb.at[zi], rsb.at[z], rsb_s.at[zi], rsb_r.at[z], {"ref": 2 * zi + x}).start()

        return c

    def arrive(i, c):
        zi = column(i)
        j = 2 * zi + x
        to_partner(whole, j, zi).wait_recv()
        to_partner(straight, j, zi).start()
        along(whole, j, zi, ag_up, ag_dn, ag_r.at[j])

        @pl.when(i >= 2)
        def _():
            take_turned(i - 1)
            other_column(i - 1, 0)

        return c

    def add_partner(i, c):
        zi = column(lax.rem(i, half))

        @pl.when(i < half)
        def _():
            own_column(i)

        remote(snd1.at[zi], rs1.at[zi], rs1_s.at[zi], rs1_r.at[zi], {"ref": partner}).wait_recv()
        for t in range(texts):
            keep[zi, t, :, hb:] = keep[zi, t, :, hb:] + decoded(rs1[zi, t], scale1)

        @pl.when(i < half)
        def _():
            for t in range(texts):
                snd2[zi, t] = coded(keep[zi, t], scale2)
            remote(snd2.at[zi], rs2.at[z], rs2_s.at[zi], rs2_r.at[z], {"ref": 2 * zi + x}).start()

        return c

    def add_turned(k, c):
        zi = lax.rem(z + k, half)
        remote(sndb.at[zi], rsb.at[zi], rsb_s.at[zi], rsb_r.at[zi], {"ref": 2 * zi + x}).wait_recv()
        for t in range(texts):
            rowb[t] = rowb[t] + decoded(rsb[zi, t], scale1)
        return c

    def gather(k, c):
        zi = lax.rem(z + k, half)
        remote(snd2.at[zi], rs2.at[zi], rs2_s.at[zi], rs2_r.at[zi], {"ref": 2 * zi + x}).wait_recv()
        for t in range(texts):
            keep[z, t] = keep[z, t] + decoded(rs2[zi, t], scale2)
        return c

    own_column(jnp.int32(0))
    to_partner(whole, 2 * z + 1 - x, z).wait_recv()
    pass_turned(z)
    lax.fori_loop(1, half, arrive, 0)
    take_turned(jnp.int32(half - 1))
    lax.fori_loop(half - 1, half + 1, other_column, 0)
    lax.fori_loop(1, half + 1, add_partner, 0)
    lax.fori_loop(1, half, add_turned, 0)
    for t in range(texts):
        sndf[t] = coded(rowb[t], scale3)
    last = remote(sndf, rsf, rsf_s, rsf_r, {"ref": partner})
    last.start()
    lax.fori_loop(1, half, gather, 0)
    last.wait_recv()
    for t in range(texts):
        keep[z, t, :, :hb] = keep[z, t, :, :hb] + decoded(rsf[t], scale3)

    first_column = (mv * n + me) * piece
    at_column = lax.broadcasted_iota(jnp.int32, (pos, piece), 1) + first_column
    at_pos = lax.broadcasted_iota(jnp.int32, (pos, 1), 0)
    lse_all = jnp.zeros((pos, LANES), f32)
    picked_all = jnp.zeros((pos, LANES), f32)
    for t in range(texts):
        both = keep[z, t]
        summed = jnp.concatenate([both[:pos], both[pos:]], axis=1)
        summed = pltpu.roll(summed, lax.rem(wl - shift, wl), 1)[:, :piece]
        root = jnp.sqrt(jnp.full((pos, LANES), counts[t].astype(f32), f32))
        factor = (1.0 / (clip_bound * root))[:, :1]
        combined = pub[t].astype(f32) + summed * factor + noise[t].astype(f32)
        combined_out[t] = combined
        peak = jnp.max(combined, axis=1, keepdims=True)
        total = jnp.sum(jnp.exp(combined - peak), axis=1, keepdims=True)
        token = jnp.zeros((pos, 1), jnp.int32)
        for p in range(pos):
            token = jnp.where(at_pos == p, tokens[t, p], token)
        picked = jnp.sum(jnp.where(at_column == token, combined, 0.0), axis=1, keepdims=True)
        lse_all = jnp.where(lane4 == t, peak + jnp.log(total), lse_all)
        picked_all = jnp.where(lane4 == t, picked, picked_all)

    out = pltpu.make_async_copy(combined_out, combined_hbm, out_sem)
    out.start()

    def exchange(slots, send, recv, index, count, axis, lse, picked):
        slots[index, :pos] = lse
        slots[index, pos:2 * pos] = picked

        def send_one(k, c):
            remote(slots.at[index], slots.at[index], send, recv, {axis: lax.rem(index + k, count)}).start()
            return c

        lax.fori_loop(1, count, send_one, 0)
        others = slots.at[pl.ds(0, count - 1)]
        pltpu.make_async_copy(others, others, recv).wait()
        pltpu.make_async_copy(others, others, send).wait()
        top = lax.fori_loop(1, count, lambda j, a: jnp.maximum(a, slots[j, :pos]), slots[0, :pos])
        zero = jnp.zeros((pos, LANES), f32)
        total, found = lax.fori_loop(
            0, count,
            lambda j, a: (a[0] + jnp.exp(slots[j, :pos] - top), a[1] + slots[j, pos:2 * pos]),
            (zero, zero),
        )
        return top + jnp.log(total), found

    lse, picked = exchange(st1, st1_s, st1_r, mv, nv, "voc", lse_all, picked_all)
    lse, picked = exchange(st2, st2_s, st2_r, me, n, "ref", lse, picked)
    stats_out[0] = lse
    stats_out[1] = picked
    out.wait()

    def left(src, sem):
        remote(src, src, sem, ag_r.at[me], {"ref": partner}).wait_send()

    def sent(i, c):
        left(snd1.at[i], rs1_s.at[i])

        @pl.when((i <= z) & (z < half - 1))
        def _():
            left(whole(me), ag_up.at[i])
            left(turning(me), agb_up.at[i])

        @pl.when((i >= z) & (z > 0))
        def _():
            left(whole(me), ag_dn.at[i])
            left(turning(me), agb_dn.at[i])

        @pl.when(i != z)
        def _():
            left(straight(me), ag_x.at[i])
            left(snd2.at[i], rs2_s.at[i])
            left(sndb.at[i], rsb_s.at[i])

        return c

    left(whole(me), ag_x.at[z])
    left(sndf, rsf_s)
    lax.fori_loop(0, half, sent, 0)


def finish(texts, pos, combined, stats, logprobs, target):
    lse = stats[0]
    score = stats[1] - lse
    at_pos = lax.broadcasted_iota(jnp.int32, (pos, pos), 0)
    at_lane = lax.broadcasted_iota(jnp.int32, (pos, pos), 1)
    for t in range(texts):
        logprobs[t] = combined[t] - lse[:, t:t + 1]
        column = jnp.where(at_pos == at_lane, score[:, t:t + 1], 0.0)
        target[t:t + 1, :] = jnp.sum(column, axis=0, keepdims=True)


def body(n, nv, private_logits, public_logits, noise, owner, counts, tokens):
    rows, pos, width = private_logits.shape
    texts, _, piece = public_logits.shape
    half = n // 2
    full = width // LANES
    win = max(-(-((j * piece) % LANES + piece) // LANES) for j in range(n))
    while min(j * piece - LANES * min(j * piece // LANES, full + 1 - win) for j in range(n)) < 0:
        win += 1
    win += win % 2
    wl = win * LANES
    hl = wl // 2
    hb = turned(win // 2) * LANES
    bf16, f32, i16 = jnp.bfloat16, jnp.float32, jnp.int16
    smem = pl.BlockSpec(memory_space=pltpu.SMEM)
    vmem = pl.BlockSpec(memory_space=pltpu.VMEM)
    dma = pltpu.SemaphoreType.DMA
    combined, stats = pl.pallas_call(
        functools.partial(kernel, n, nv, rows, texts, pos, width, piece, win),
        out_shape=(
            jax.ShapeDtypeStruct((texts, pos, piece), f32),
            jax.ShapeDtypeStruct((2, pos, LANES), f32),
        ),
        in_specs=[smem, smem, smem, pl.BlockSpec(memory_space=pl.ANY), vmem, vmem],
        out_specs=(pl.BlockSpec(memory_space=pl.ANY), vmem),
        scratch_shapes=[
            pltpu.VMEM((texts, pos, piece), f32),
            pltpu.VMEM((rows, pos, width), bf16),
            pltpu.VMEM((rows, pos, n * LANES), bf16),
            pltpu.VMEM((texts, pos, wl), f32),
            pltpu.VMEM((n, texts, 2 * pos, hl), bf16),
            pltpu.VMEM((texts, 2 * pos, hl), f32),
            pltpu.VMEM((rows + 1, 2 * pos, hl), f32),
            pltpu.VMEM((half, texts, 2 * pos, hl), f32),
            pltpu.VMEM((half, texts, 2 * pos, hl - hb), i16),
            pltpu.VMEM((half, texts, 2 * pos, hl - hb), i16),
            pltpu.VMEM((half, texts, 2 * pos, hl), i16),
            pltpu.VMEM((half, texts, 2 * pos, hl), i16),
            pltpu.VMEM((texts, 2 * pos, hb), f32),
            pltpu.VMEM((half, texts, 2 * pos, hb), i16),
            pltpu.VMEM((half, texts, 2 * pos, hb), i16),
            pltpu.VMEM((texts, 2 * pos, hb), i16),
            pltpu.VMEM((texts, 2 * pos, hb), i16),
            pltpu.VMEM((n, 2 * pos, LANES), jnp.int32),
            pltpu.VMEM((nv, 2 * pos, LANES), f32),
            pltpu.VMEM((n, 2 * pos, LANES), f32),
            pltpu.VMEM((rows, 2 * pos, LANES), f32),
            pltpu.SMEM((rows,), jnp.int32),
            pltpu.SMEM((rows,), jnp.int32),
            pltpu.SMEM((texts + 1,), jnp.int32),
            dma, dma, dma,
            dma((half,)), dma((half,)), dma((half,)), dma((n,)),
            dma((half,)), dma((half,)), dma((half,)),
            dma((half,)), dma((half,)), dma((half,)), dma((half,)),
            dma((half,)), dma((half,)), dma, dma,
            dma, dma, dma, dma, dma,
        ],
        compiler_params=pltpu.CompilerParams(
            collective_id=0, has_side_effects=True, vmem_limit_bytes=56 * 1024 * 1024
        ),
        cost_estimate=pl.CostEstimate(
            flops=6 * rows * pos * width, bytes_accessed=2 * rows * pos * width, transcendentals=0
        ),
        name="private_scores",
    )(owner, counts, tokens, private_logits, public_logits, noise)
    return pl.pallas_call(
        functools.partial(finish, texts, pos),
        out_shape=(
            jax.ShapeDtypeStruct((texts, pos, piece), f32),
            jax.ShapeDtypeStruct((texts, pos), f32),
        ),
        in_specs=[vmem, vmem],
        out_specs=(vmem, vmem),
        name="subtract_lse",
    )(combined, stats)


def solution(mesh):
    return jax.shard_map(
        functools.partial(body, mesh.shape["ref"], mesh.shape["voc"]),
        mesh=mesh,
        in_specs=(
            P("ref", None, "voc"),
            P(None, None, ("voc", "ref")),
            P(None, None, ("voc", "ref")),
            P("ref"),
            P(),
            P(),
        ),
        out_specs=(P(None, None, ("voc", "ref")), P()),
        check_vma=False,
    )
```

```python
import functools

import jax
import jax.numpy as jnp
from jax import lax
from jax.experimental import pallas as pl
from jax.experimental.pallas import tpu as pltpu
from jax.sharding import PartitionSpec as P

clip_bound = 2.0
LANES = 128
MESH = pl.DeviceIdType.MESH


def fixed_point(rows):
    scale = 1
    while scale * 2 * clip_bound * rows <= 32000:
        scale *= 2
    return float(scale)


def turned(pairs):
    return (pairs + 3) // 6


def kernel(
    n, nv, rows, texts, pos, width, piece, win,
    owner, counts, tokens, priv, pub, noise,
    combined_hbm, stats_out,
    combined_out,    pv, xt, pubf, pubs, here, pref, keep, snd1, rs1, snd2, rs2, rowb, sndb, rsb, sndf, rsf,
    hist, st1, st2, bnd, order, sown, start,
    priv_sem, hist_s, hist_r, ag_x, ag_up, ag_dn, ag_r, agb_up, agb_dn, agb_r,
    rs1_s, rs1_r, rs2_s, rs2_r, rsb_s, rsb_r, rsf_s, rsf_r,
    st1_s, st1_r, st2_s, st2_r, out_sem,
):
    f32 = jnp.float32
    half = n // 2
    full = width // LANES
    wl = win * LANES
    pairs = win // 2
    hl = pairs * LANES
    hb = turned(pairs) * LANES
    me = lax.axis_index("ref")
    mv = lax.axis_index("voc")
    z = lax.div(me, 2)
    x = lax.rem(me, 2)
    partner = me + 1 - 2 * x
    scale1 = fixed_point(rows)
    scale2 = fixed_point(min(2 * rows, n * rows // texts))
    scale3 = fixed_point(min(half * rows, n * rows // texts))

    def first_tile(j):
        return jnp.minimum(lax.div(j * piece, LANES), full + 1 - win)

    def remote(src, dst, send, recv, peer):
        return pltpu.make_async_remote_copy(
            src_ref=src, dst_ref=dst, send_sem=send, recv_sem=recv,
            device_id=peer, device_id_type=MESH,
        )

    load = pltpu.make_async_copy(priv, pv, priv_sem)
    load.start()
    barrier = pltpu.get_barrier_semaphore()

    def greet(k, c):
        pl.semaphore_signal(barrier, inc=1, device_id={"ref": lax.rem(me + k, n)}, device_id_type=MESH)
        return c

    def greet_voc(k, c):
        pl.semaphore_signal(barrier, inc=1, device_id={"voc": lax.rem(mv + k, nv)}, device_id_type=MESH)
        return c

    lax.fori_loop(1, n, greet, 0)
    lax.fori_loop(1, nv, greet_voc, 0)

    shift = me * piece - first_tile(me) * LANES
    pubf[...] = jnp.zeros_like(pubf)
    for t in range(texts):
        pubf[t, :, :piece] = pub[t].astype(f32)
    for t in range(texts):
        moved = pltpu.roll(pubf[t], shift, 1)
        pubs[me, t] = jnp.concatenate([moved[:, :hl], moved[:, hl:]], axis=0).astype(jnp.bfloat16)

    own = [owner[r] for r in range(rows)]
    hits = [sum((o == t).astype(jnp.int32) for o in own) for t in range(texts)]
    lane8 = lax.broadcasted_iota(jnp.int32, (2 * pos, LANES), 1)
    mine = jnp.zeros((2 * pos, LANES), jnp.int32)
    for t in range(texts):
        mine = jnp.where(lane8 == t, hits[t], mine)
    hist[me] = mine

    pl.semaphore_wait(barrier, n - 1 + nv - 1)

    def whole(j):
        return pubs.at[j]

    def straight(j):
        return pubs.at[j, :, :, pl.ds(hb, hl - hb)]

    def turning(j):
        return pubs.at[j, :, :, pl.ds(0, hb)]

    def to_partner(part, j, zi):
        return remote(part(j), part(j), ag_x.at[zi], ag_r.at[j], {"ref": partner})

    def along(part, j, zi, up, down, recv):
        @pl.when((zi <= z) & (z < half - 1))
        def _():
            remote(part(j), part(j), up.at[zi], recv, {"ref": me + 2}).start()

        @pl.when((zi >= z) & (z > 0))
        def _():
            remote(part(j), part(j), down.at[zi], recv, {"ref": me - 2}).start()

    def pass_turned(zi):
        j = 2 * zi + 1 - x
        along(turning, j, zi, agb_up, agb_dn, agb_r.at[zi])

    def send_hist(k, c):
        remote(hist.at[me], hist.at[me], hist_s, hist_r, {"ref": lax.rem(me + k, n)}).start()
        return c

    lax.fori_loop(1, n, send_hist, 0)
    to_partner(whole, me, z).start()
    along(whole, me, z, ag_up, ag_dn, ag_r.at[me])

    begin = [jnp.int32(0)]
    for t in range(texts):
        begin.append(begin[-1] + hits[t])
    for t in range(texts + 1):
        start[t] = begin[t]
    place = []
    for r in range(rows):
        before = jnp.int32(0)
        for q in range(rows):
            if q < r:
                before = before + (own[q] <= own[r]).astype(jnp.int32)
            elif q > r:
                before = before + (own[q] < own[r]).astype(jnp.int32)
        place.append(before)
    for k in range(rows):
        at = jnp.int32(0)
        for r in range(rows):
            at = at + jnp.where(place[r] == k, r, 0)
        order[k] = at
        sown[k] = sum((begin[t] <= k).astype(jnp.int32) for t in range(1, texts))

    def partial_sums(j, store):
        base = first_tile(j) * LANES
        for t in range(texts):
            here[t] = pubs[j, t].astype(f32)
        base = pl.multiple_of(base, LANES)
        middle = pl.multiple_of(base + hl, LANES)
        end = pl.multiple_of(j * LANES, LANES)
        acc = jnp.zeros((2 * pos, hl), f32)
        for k in range(rows):
            row = order[k]
            b = jnp.concatenate([bnd[k]] * pairs, axis=1)
            low = pv[row, :, pl.ds(base, hl)].astype(f32)
            high = pv[row, :, pl.ds(middle, hl - LANES)].astype(f32)
            high = jnp.concatenate([high, xt[row, :, pl.ds(end, LANES)].astype(f32)], axis=1)
            p = jnp.concatenate([low, high], axis=0)
            acc = acc + jnp.minimum(jnp.maximum(p - here[sown[k]], -b), b)
            pref[k + 1] = acc
        for t in range(texts):
            store(t, pref[start[t + 1]] - pref[start[t]])

    def coded(v, scale):
        return jnp.round(v * scale).astype(jnp.int32).astype(jnp.int16)

    def decoded(q, scale):
        return q.astype(jnp.int32).astype(f32) * (1.0 / scale)

    nearer = jnp.minimum(z, half - 1 - z)

    def column(i):
        side = jnp.where(lax.rem(i, 2) == 1, -lax.div(i + 1, 2), lax.div(i, 2))
        rest = jnp.where(z < half - 1 - z, i, half - 1 - i)
        return jnp.where(i <= 2 * nearer, z + side, rest)

    def own_column(i):
        zi = column(i)

        def store(t, v):
            keep[zi, t] = v

        partial_sums(2 * zi + x, store)

    def take_turned(i):
        zi = column(i)
        part = turning(2 * zi + 1 - x)
        remote(part, part, agb_up.at[zi], agb_r.at[zi], {"ref": partner}).wait_recv()
        pass_turned(zi)

    def other_column(i, c):
        zi = column(lax.rem(i, half))
        j = 2 * zi + 1 - x

        @pl.when(i < half)
        def _():
            to_partner(straight, j, zi).wait_recv()

        def store(t, v):
            snd1[zi, t] = coded(v[:, hb:], scale1)
            sndb[zi, t] = coded(v[:, :hb], scale1)
            rowb[t] = v[:, :hb]

        partial_sums(j, store)
        remote(snd1.at[zi], rs1.at[zi], rs1_s.at[zi], rs1_r.at[zi], {"ref": partner}).start()

        @pl.when(i < half)
        def _():
            remote(sndb.at[zi], rsb.at[z], rsb_s.at[zi], rsb_r.at[z], {"ref": 2 * zi + x}).start()

        return c

    def arrive(i, c):
        zi = column(i)
        j = 2 * zi + x
        to_partner(whole, j, zi).wait_recv()
        to_partner(straight, j, zi).start()
        along(whole, j, zi, ag_up, ag_dn, ag_r.at[j])

        @pl.when(i >= 2)
        def _():
            take_turned(i - 1)
            other_column(i - 1, 0)

        return c

    def add_partner(i, c):
        zi = column(lax.rem(i, half))
        own_column(lax.rem(i, half))
        remote(snd1.at[zi], rs1.at[zi], rs1_s.at[zi], rs1_r.at[zi], {"ref": partner}).wait_recv()
        for t in range(texts):
            keep[zi, t, :, hb:] = keep[zi, t, :, hb:] + decoded(rs1[zi, t], scale1)

        @pl.when(i < half)
        def _():
            for t in range(texts):
                snd2[zi, t] = coded(keep[zi, t], scale2)
            remote(snd2.at[zi], rs2.at[z], rs2_s.at[zi], rs2_r.at[z], {"ref": 2 * zi + x}).start()

        return c

    def add_turned(k, c):
        zi = lax.rem(z + k, half)
        remote(sndb.at[zi], rsb.at[zi], rsb_s.at[zi], rsb_r.at[zi], {"ref": 2 * zi + x}).wait_recv()
        for t in range(texts):
            rowb[t] = rowb[t] + decoded(rsb[zi, t], scale1)
        return c

    def gather(k, c):
        zi = lax.rem(z + k, half)
        remote(snd2.at[zi], rs2.at[zi], rs2_s.at[zi], rs2_r.at[zi], {"ref": 2 * zi + x}).wait_recv()
        for t in range(texts):
            keep[z, t] = keep[z, t] + decoded(rs2[zi, t], scale2)
        return c

    to_partner(whole, 2 * z + 1 - x, z).wait_recv()
    pass_turned(z)
    arrive(jnp.int32(1), 0)

    load.wait()
    for j in range(n):
        s = min(j * piece // LANES, full + 1 - win) + win - 1
        if s < full:
            xt[:, :, j * LANES:(j + 1) * LANES] = pv[:, :, s * LANES:(s + 1) * LANES]
        else:
            xt[:, :, j * LANES:(j + 1) * LANES] = jnp.zeros((rows, pos, LANES), jnp.bfloat16)
            if width > full * LANES:
                xt[:, :, j * LANES:j * LANES + width - full * LANES] = pv[:, :, full * LANES:]

    got = hist.at[pl.ds(0, n - 1)]
    pltpu.make_async_copy(got, got, hist_r).wait()
    pltpu.make_async_copy(got, got, hist_s).wait()
    lower = jnp.zeros((2 * pos, LANES), jnp.int32)
    lower = lax.fori_loop(0, n, lambda j, a: a + jnp.where(j < me, hist[j], 0), lower)
    lane4 = lane8[:pos]
    pref[0] = jnp.zeros_like(pref[0])
    for k in range(rows):
        text = sown[k]
        limit = counts[text] - (k - start[text])
        ok = jnp.where((lane8 == text) & (lower < limit), clip_bound, 0.0)
        bnd[k] = jnp.broadcast_to(jnp.max(ok, axis=1, keepdims=True), (2 * pos, LANES))

    lax.fori_loop(2, half, arrive, 0)
    take_turned(jnp.int32(half - 1))
    lax.fori_loop(half - 1, half + 1, other_column, 0)
    lax.fori_loop(1, half + 1, add_partner, 0)
    lax.fori_loop(1, half, add_turned, 0)
    for t in range(texts):
        sndf[t] = coded(rowb[t], scale3)
    last = remote(sndf, rsf, rsf_s, rsf_r, {"ref": partner})
    last.start()
    lax.fori_loop(1, half, gather, 0)
    last.wait_recv()
    for t in range(texts):
        keep[z, t, :, :hb] = keep[z, t, :, :hb] + decoded(rsf[t], scale3)

    first_column = (mv * n + me) * piece
    at_column = lax.broadcasted_iota(jnp.int32, (pos, piece), 1) + first_column
    at_pos = lax.broadcasted_iota(jnp.int32, (pos, 1), 0)
    lse_all = jnp.zeros((pos, LANES), f32)
    picked_all = jnp.zeros((pos, LANES), f32)
    for t in range(texts):
        both = keep[z, t]
        summed = jnp.concatenate([both[:pos], both[pos:]], axis=1)
        summed = pltpu.roll(summed, lax.rem(wl - shift, wl), 1)[:, :piece]
        root = jnp.sqrt(jnp.full((pos, LANES), counts[t].astype(f32), f32))
        factor = (1.0 / (clip_bound * root))[:, :1]
        combined = pub[t].astype(f32) + summed * factor + noise[t].astype(f32)
        combined_out[t] = combined
        peak = jnp.max(combined, axis=1, keepdims=True)
        total = jnp.sum(jnp.exp(combined - peak), axis=1, keepdims=True)
        token = jnp.zeros((pos, 1), jnp.int32)
        for p in range(pos):
            token = jnp.where(at_pos == p, tokens[t, p], token)
        picked = jnp.sum(jnp.where(at_column == token, combined, 0.0), axis=1, keepdims=True)
        lse_all = jnp.where(lane4 == t, peak + jnp.log(total), lse_all)
        picked_all = jnp.where(lane4 == t, picked, picked_all)

    out = pltpu.make_async_copy(combined_out, combined_hbm, out_sem)
    out.start()

    def exchange(slots, send, recv, index, count, axis, lse, picked):
        slots[index, :pos] = lse
        slots[index, pos:2 * pos] = picked

        def send_one(k, c):
            remote(slots.at[index], slots.at[index], send, recv, {axis: lax.rem(index + k, count)}).start()
            return c

        lax.fori_loop(1, count, send_one, 0)
        others = slots.at[pl.ds(0, count - 1)]
        pltpu.make_async_copy(others, others, recv).wait()
        pltpu.make_async_copy(others, others, send).wait()
        top = lax.fori_loop(1, count, lambda j, a: jnp.maximum(a, slots[j, :pos]), slots[0, :pos])
        zero = jnp.zeros((pos, LANES), f32)
        total, found = lax.fori_loop(
            0, count,
            lambda j, a: (a[0] + jnp.exp(slots[j, :pos] - top), a[1] + slots[j, pos:2 * pos]),
            (zero, zero),
        )
        return top + jnp.log(total), found

    lse, picked = exchange(st1, st1_s, st1_r, mv, nv, "voc", lse_all, picked_all)
    lse, picked = exchange(st2, st2_s, st2_r, me, n, "ref", lse, picked)
    stats_out[0] = lse
    stats_out[1] = picked
    out.wait()

    def left(src, sem):
        remote(src, src, sem, ag_r.at[me], {"ref": partner}).wait_send()

    def sent(i, c):
        left(snd1.at[i], rs1_s.at[i])

        @pl.when((i <= z) & (z < half - 1))
        def _():
            left(whole(me), ag_up.at[i])
            left(turning(me), agb_up.at[i])

        @pl.when((i >= z) & (z > 0))
        def _():
            left(whole(me), ag_dn.at[i])
            left(turning(me), agb_dn.at[i])

        @pl.when(i != z)
        def _():
            left(straight(me), ag_x.at[i])
            left(snd2.at[i], rs2_s.at[i])
            left(sndb.at[i], rsb_s.at[i])

        return c

    left(whole(me), ag_x.at[z])
    left(sndf, rsf_s)
    lax.fori_loop(0, half, sent, 0)


def finish(texts, pos, combined, stats, logprobs, target):
    lse = stats[0]
    score = stats[1] - lse
    at_pos = lax.broadcasted_iota(jnp.int32, (pos, pos), 0)
    at_lane = lax.broadcasted_iota(jnp.int32, (pos, pos), 1)
    for t in range(texts):
        logprobs[t] = combined[t] - lse[:, t:t + 1]
        column = jnp.where(at_pos == at_lane, score[:, t:t + 1], 0.0)
        target[t:t + 1, :] = jnp.sum(column, axis=0, keepdims=True)


def body(n, nv, private_logits, public_logits, noise, owner, counts, tokens):
    rows, pos, width = private_logits.shape
    texts, _, piece = public_logits.shape
    half = n // 2
    full = width // LANES
    win = max(-(-((j * piece) % LANES + piece) // LANES) for j in range(n))
    while min(j * piece - LANES * min(j * piece // LANES, full + 1 - win) for j in range(n)) < 0:
        win += 1
    win += win % 2
    wl = win * LANES
    hl = wl // 2
    hb = turned(win // 2) * LANES
    bf16, f32, i16 = jnp.bfloat16, jnp.float32, jnp.int16
    smem = pl.BlockSpec(memory_space=pltpu.SMEM)
    vmem = pl.BlockSpec(memory_space=pltpu.VMEM)
    dma = pltpu.SemaphoreType.DMA
    combined, stats = pl.pallas_call(
        functools.partial(kernel, n, nv, rows, texts, pos, width, piece, win),
        out_shape=(
            jax.ShapeDtypeStruct((texts, pos, piece), f32),
            jax.ShapeDtypeStruct((2, pos, LANES), f32),
        ),
        in_specs=[smem, smem, smem, pl.BlockSpec(memory_space=pl.ANY), vmem, vmem],
        out_specs=(pl.BlockSpec(memory_space=pl.ANY), vmem),
        scratch_shapes=[
            pltpu.VMEM((texts, pos, piece), f32),
            pltpu.VMEM((rows, pos, width), bf16),
            pltpu.VMEM((rows, pos, n * LANES), bf16),
            pltpu.VMEM((texts, pos, wl), f32),
            pltpu.VMEM((n, texts, 2 * pos, hl), bf16),
            pltpu.VMEM((texts, 2 * pos, hl), f32),
            pltpu.VMEM((rows + 1, 2 * pos, hl), f32),
            pltpu.VMEM((half, texts, 2 * pos, hl), f32),
            pltpu.VMEM((half, texts, 2 * pos, hl - hb), i16),
            pltpu.VMEM((half, texts, 2 * pos, hl - hb), i16),
            pltpu.VMEM((half, texts, 2 * pos, hl), i16),
            pltpu.VMEM((half, texts, 2 * pos, hl), i16),
            pltpu.VMEM((texts, 2 * pos, hb), f32),
            pltpu.VMEM((half, texts, 2 * pos, hb), i16),
            pltpu.VMEM((half, texts, 2 * pos, hb), i16),
            pltpu.VMEM((texts, 2 * pos, hb), i16),
            pltpu.VMEM((texts, 2 * pos, hb), i16),
            pltpu.VMEM((n, 2 * pos, LANES), jnp.int32),
            pltpu.VMEM((nv, 2 * pos, LANES), f32),
            pltpu.VMEM((n, 2 * pos, LANES), f32),
            pltpu.VMEM((rows, 2 * pos, LANES), f32),
            pltpu.SMEM((rows,), jnp.int32),
            pltpu.SMEM((rows,), jnp.int32),
            pltpu.SMEM((texts + 1,), jnp.int32),
            dma, dma, dma,
            dma((half,)), dma((half,)), dma((half,)), dma((n,)),
            dma((half,)), dma((half,)), dma((half,)),
            dma((half,)), dma((half,)), dma((half,)), dma((half,)),
            dma((half,)), dma((half,)), dma, dma,
            dma, dma, dma, dma, dma,
        ],
        compiler_params=pltpu.CompilerParams(
            collective_id=0, has_side_effects=True, vmem_limit_bytes=56 * 1024 * 1024
        ),
        cost_estimate=pl.CostEstimate(
            flops=6 * rows * pos * width, bytes_accessed=2 * rows * pos * width, transcendentals=0
        ),
        name="private_scores",
    )(owner, counts, tokens, private_logits, public_logits, noise)
    return pl.pallas_call(
        functools.partial(finish, texts, pos),
        out_shape=(
            jax.ShapeDtypeStruct((texts, pos, piece), f32),
            jax.ShapeDtypeStruct((texts, pos), f32),
        ),
        in_specs=[vmem, vmem],
        out_specs=(vmem, vmem),
        name="subtract_lse",
    )(combined, stats)


def solution(mesh):
    return jax.shard_map(
        functools.partial(body, mesh.shape["ref"], mesh.shape["voc"]),
        mesh=mesh,
        in_specs=(
            P("ref", None, "voc"),
            P(None, None, ("voc", "ref")),
            P(None, None, ("voc", "ref")),
            P("ref"),
            P(),
            P(),
        ),
        out_specs=(P(None, None, ("voc", "ref")), P()),
        check_vma=False,
    )
```

```python
import functools

import jax
import jax.numpy as jnp
from jax import lax
from jax.experimental import pallas as pl
from jax.experimental.pallas import tpu as pltpu
from jax.sharding import PartitionSpec as P

clip_bound = 2.0
LANES = 128
MESH = pl.DeviceIdType.MESH


def fixed_point(rows):
    scale = 1
    while scale * 2 * clip_bound * rows <= 32000:
        scale *= 2
    return float(scale)


def turned(pairs):
    return (pairs + 3) // 6


def kernel(
    n, nv, rows, texts, pos, width, piece, win,
    owner, counts, tokens, priv, pub, noise,
    combined_hbm, stats_out,
    combined_out,    pv, xt, pubf, pubs, here, pref, keep, snd1, rs1, snd2, rs2,
    hist, st1, st2, bnd, order, sown, start,
    priv_sem, hist_s, hist_r, ag_x, ag_up, ag_dn, ag_r, agb_up, agb_dn, agb_r,
    rs1_s, rs1_r, rs2_s, rs2_r,
    st1_s, st1_r, st2_s, st2_r, out_sem,
):
    f32 = jnp.float32
    half = n // 2
    full = width // LANES
    wl = win * LANES
    pairs = win // 2
    hl = pairs * LANES
    hb = turned(pairs) * LANES
    me = lax.axis_index("ref")
    mv = lax.axis_index("voc")
    z = lax.div(me, 2)
    x = lax.rem(me, 2)
    partner = me + 1 - 2 * x
    scale1 = fixed_point(rows)
    scale2 = fixed_point(min(2 * rows, n * rows // texts))

    def first_tile(j):
        return jnp.minimum(lax.div(j * piece, LANES), full + 1 - win)

    def remote(src, dst, send, recv, peer):
        return pltpu.make_async_remote_copy(
            src_ref=src, dst_ref=dst, send_sem=send, recv_sem=recv,
            device_id=peer, device_id_type=MESH,
        )

    load = pltpu.make_async_copy(priv, pv, priv_sem)
    load.start()
    barrier = pltpu.get_barrier_semaphore()

    def greet(k, c):
        pl.semaphore_signal(barrier, inc=1, device_id={"ref": lax.rem(me + k, n)}, device_id_type=MESH)
        return c

    def greet_voc(k, c):
        pl.semaphore_signal(barrier, inc=1, device_id={"voc": lax.rem(mv + k, nv)}, device_id_type=MESH)
        return c

    lax.fori_loop(1, n, greet, 0)
    lax.fori_loop(1, nv, greet_voc, 0)

    shift = me * piece - first_tile(me) * LANES
    pubf[...] = jnp.zeros_like(pubf)
    for t in range(texts):
        pubf[t, :, :piece] = pub[t].astype(f32)
    for t in range(texts):
        moved = pltpu.roll(pubf[t], shift, 1)
        pubs[me, t] = jnp.concatenate([moved[:, :hl], moved[:, hl:]], axis=0).astype(jnp.bfloat16)

    own = [owner[r] for r in range(rows)]
    hits = [sum((o == t).astype(jnp.int32) for o in own) for t in range(texts)]
    lane8 = lax.broadcasted_iota(jnp.int32, (2 * pos, LANES), 1)
    mine = jnp.zeros((2 * pos, LANES), jnp.int32)
    for t in range(texts):
        mine = jnp.where(lane8 == t, hits[t], mine)
    hist[me] = mine

    pl.semaphore_wait(barrier, n - 1 + nv - 1)

    def whole(j):
        return pubs.at[j]

    def straight(j):
        return pubs.at[j, :, :, pl.ds(hb, hl - hb)]

    def turning(j):
        return pubs.at[j, :, :, pl.ds(0, hb)]

    def to_partner(part, j, zi):
        return remote(part(j), part(j), ag_x.at[zi], ag_r.at[j], {"ref": partner})

    def along(part, j, zi, up, down, recv):
        @pl.when((zi <= z) & (z < half - 1))
        def _():
            remote(part(j), part(j), up.at[zi], recv, {"ref": me + 2}).start()

        @pl.when((zi >= z) & (z > 0))
        def _():
            remote(part(j), part(j), down.at[zi], recv, {"ref": me - 2}).start()

    def pass_turned(zi):
        j = 2 * zi + 1 - x
        along(turning, j, zi, agb_up, agb_dn, agb_r.at[zi])

    def send_hist(k, c):
        remote(hist.at[me], hist.at[me], hist_s, hist_r, {"ref": lax.rem(me + k, n)}).start()
        return c

    lax.fori_loop(1, n, send_hist, 0)
    to_partner(whole, me, z).start()
    along(whole, me, z, ag_up, ag_dn, ag_r.at[me])

    begin = [jnp.int32(0)]
    for t in range(texts):
        begin.append(begin[-1] + hits[t])
    for t in range(texts + 1):
        start[t] = begin[t]
    place = []
    for r in range(rows):
        before = jnp.int32(0)
        for q in range(rows):
            if q < r:
                before = before + (own[q] <= own[r]).astype(jnp.int32)
            elif q > r:
                before = before + (own[q] < own[r]).astype(jnp.int32)
        place.append(before)
    for k in range(rows):
        at = jnp.int32(0)
        for r in range(rows):
            at = at + jnp.where(place[r] == k, r, 0)
        order[k] = at
        sown[k] = sum((begin[t] <= k).astype(jnp.int32) for t in range(1, texts))

    def partial_sums(j, store):
        base = first_tile(j) * LANES
        for t in range(texts):
            here[t] = pubs[j, t].astype(f32)
        base = pl.multiple_of(base, LANES)
        middle = pl.multiple_of(base + hl, LANES)
        end = pl.multiple_of(j * LANES, LANES)
        acc = jnp.zeros((2 * pos, hl), f32)
        for k in range(rows):
            row = order[k]
            b = jnp.concatenate([bnd[k]] * pairs, axis=1)
            low = pv[row, :, pl.ds(base, hl)].astype(f32)
            high = pv[row, :, pl.ds(middle, hl - LANES)].astype(f32)
            high = jnp.concatenate([high, xt[row, :, pl.ds(end, LANES)].astype(f32)], axis=1)
            p = jnp.concatenate([low, high], axis=0)
            acc = acc + jnp.minimum(jnp.maximum(p - here[sown[k]], -b), b)
            pref[k + 1] = acc
        for t in range(texts):
            store(t, pref[start[t + 1]] - pref[start[t]])

    def coded(v, scale):
        return jnp.round(v * scale).astype(jnp.int32).astype(jnp.int16)

    def decoded(q, scale):
        return q.astype(jnp.int32).astype(f32) * (1.0 / scale)

    nearer = jnp.minimum(z, half - 1 - z)

    def column(i):
        side = jnp.where(lax.rem(i, 2) == 1, -lax.div(i + 1, 2), lax.div(i, 2))
        rest = jnp.where(z < half - 1 - z, i, half - 1 - i)
        return jnp.where(i <= 2 * nearer, z + side, rest)

    def own_column(i):
        zi = column(i)

        def store(t, v):
            keep[zi, t] = v

        partial_sums(2 * zi + x, store)

    def take_turned(i):
        zi = column(i)
        part = turning(2 * zi + 1 - x)
        remote(part, part, agb_up.at[zi], agb_r.at[zi], {"ref": partner}).wait_recv()
        pass_turned(zi)

    def other_column(i, c):
        zi = column(lax.rem(i, half))
        j = 2 * zi + 1 - x

        @pl.when(i < half)
        def _():
            to_partner(straight, j, zi).wait_recv()

        def store(t, v):
            snd1[zi, t] = coded(v, scale1)

        partial_sums(j, store)
        remote(snd1.at[zi], rs1.at[zi], rs1_s.at[zi], rs1_r.at[zi], {"ref": partner}).start()

        return c

    def arrive(i, c):
        zi = column(i)
        j = 2 * zi + x
        to_partner(whole, j, zi).wait_recv()
        to_partner(straight, j, zi).start()
        along(whole, j, zi, ag_up, ag_dn, ag_r.at[j])

        @pl.when(i >= 2)
        def _():
            take_turned(i - 1)
            other_column(i - 1, 0)

        return c

    def add_partner(i, c):
        zi = column(lax.rem(i, half))

        @pl.when(i < half)
        def _():
            own_column(i)

        remote(snd1.at[zi], rs1.at[zi], rs1_s.at[zi], rs1_r.at[zi], {"ref": partner}).wait_recv()
        for t in range(texts):
            keep[zi, t] = keep[zi, t] + decoded(rs1[zi, t], scale1)

        @pl.when(i < half)
        def _():
            for t in range(texts):
                snd2[zi, t] = coded(keep[zi, t], scale2)
            remote(snd2.at[zi], rs2.at[z], rs2_s.at[zi], rs2_r.at[z], {"ref": 2 * zi + x}).start()

        @pl.when(i == 1)
        def _():
            own_column(jnp.int32(0))

        return c

    def gather(k, c):
        zi = lax.rem(z + k, half)
        remote(snd2.at[zi], rs2.at[zi], rs2_s.at[zi], rs2_r.at[zi], {"ref": 2 * zi + x}).wait_recv()
        for t in range(texts):
            keep[z, t] = keep[z, t] + decoded(rs2[zi, t], scale2)
        return c

    to_partner(whole, 2 * z + 1 - x, z).wait_recv()
    pass_turned(z)
    arrive(jnp.int32(1), 0)

    load.wait()
    for j in range(n):
        s = min(j * piece // LANES, full + 1 - win) + win - 1
        if s < full:
            xt[:, :, j * LANES:(j + 1) * LANES] = pv[:, :, s * LANES:(s + 1) * LANES]
        else:
            xt[:, :, j * LANES:(j + 1) * LANES] = jnp.zeros((rows, pos, LANES), jnp.bfloat16)
            if width > full * LANES:
                xt[:, :, j * LANES:j * LANES + width - full * LANES] = pv[:, :, full * LANES:]

    got = hist.at[pl.ds(0, n - 1)]
    pltpu.make_async_copy(got, got, hist_r).wait()
    pltpu.make_async_copy(got, got, hist_s).wait()
    lower = jnp.zeros((2 * pos, LANES), jnp.int32)
    lower = lax.fori_loop(0, n, lambda j, a: a + jnp.where(j < me, hist[j], 0), lower)
    lane4 = lane8[:pos]
    pref[0] = jnp.zeros_like(pref[0])
    for k in range(rows):
        text = sown[k]
        limit = counts[text] - (k - start[text])
        ok = jnp.where((lane8 == text) & (lower < limit), clip_bound, 0.0)
        bnd[k] = jnp.broadcast_to(jnp.max(ok, axis=1, keepdims=True), (2 * pos, LANES))

    lax.fori_loop(2, half, arrive, 0)
    take_turned(jnp.int32(half - 1))
    lax.fori_loop(half - 1, half + 1, other_column, 0)
    lax.fori_loop(1, half + 1, add_partner, 0)
    lax.fori_loop(1, half, gather, 0)

    first_column = (mv * n + me) * piece
    at_column = lax.broadcasted_iota(jnp.int32, (pos, piece), 1) + first_column
    at_pos = lax.broadcasted_iota(jnp.int32, (pos, 1), 0)
    lse_all = jnp.zeros((pos, LANES), f32)
    picked_all = jnp.zeros((pos, LANES), f32)
    for t in range(texts):
        both = keep[z, t]
        summed = jnp.concatenate([both[:pos], both[pos:]], axis=1)
        summed = pltpu.roll(summed, lax.rem(wl - shift, wl), 1)[:, :piece]
        root = jnp.sqrt(jnp.full((pos, LANES), counts[t].astype(f32), f32))
        factor = (1.0 / (clip_bound * root))[:, :1]
        combined = pub[t].astype(f32) + summed * factor + noise[t].astype(f32)
        combined_out[t] = combined
        peak = jnp.max(combined, axis=1, keepdims=True)
        total = jnp.sum(jnp.exp(combined - peak), axis=1, keepdims=True)
        token = jnp.zeros((pos, 1), jnp.int32)
        for p in range(pos):
            token = jnp.where(at_pos == p, tokens[t, p], token)
        picked = jnp.sum(jnp.where(at_column == token, combined, 0.0), axis=1, keepdims=True)
        lse_all = jnp.where(lane4 == t, peak + jnp.log(total), lse_all)
        picked_all = jnp.where(lane4 == t, picked, picked_all)

    out = pltpu.make_async_copy(combined_out, combined_hbm, out_sem)
    out.start()

    def exchange(slots, send, recv, index, count, axis, lse, picked):
        slots[index, :pos] = lse
        slots[index, pos:2 * pos] = picked

        def send_one(k, c):
            remote(slots.at[index], slots.at[index], send, recv, {axis: lax.rem(index + k, count)}).start()
            return c

        lax.fori_loop(1, count, send_one, 0)
        others = slots.at[pl.ds(0, count - 1)]
        pltpu.make_async_copy(others, others, recv).wait()
        pltpu.make_async_copy(others, others, send).wait()
        top = lax.fori_loop(1, count, lambda j, a: jnp.maximum(a, slots[j, :pos]), slots[0, :pos])
        zero = jnp.zeros((pos, LANES), f32)
        total, found = lax.fori_loop(
            0, count,
            lambda j, a: (a[0] + jnp.exp(slots[j, :pos] - top), a[1] + slots[j, pos:2 * pos]),
            (zero, zero),
        )
        return top + jnp.log(total), found

    lse, picked = exchange(st1, st1_s, st1_r, mv, nv, "voc", lse_all, picked_all)
    lse, picked = exchange(st2, st2_s, st2_r, me, n, "ref", lse, picked)
    stats_out[0] = lse
    stats_out[1] = picked
    out.wait()

    def left(src, sem):
        remote(src, src, sem, ag_r.at[me], {"ref": partner}).wait_send()

    def sent(i, c):
        left(snd1.at[i], rs1_s.at[i])

        @pl.when((i <= z) & (z < half - 1))
        def _():
            left(whole(me), ag_up.at[i])
            left(turning(me), agb_up.at[i])

        @pl.when((i >= z) & (z > 0))
        def _():
            left(whole(me), ag_dn.at[i])
            left(turning(me), agb_dn.at[i])

        @pl.when(i != z)
        def _():
            left(straight(me), ag_x.at[i])
            left(snd2.at[i], rs2_s.at[i])

        return c

    left(whole(me), ag_x.at[z])
    lax.fori_loop(0, half, sent, 0)


def finish(texts, pos, combined, stats, logprobs, target):
    lse = stats[0]
    score = stats[1] - lse
    at_pos = lax.broadcasted_iota(jnp.int32, (pos, pos), 0)
    at_lane = lax.broadcasted_iota(jnp.int32, (pos, pos), 1)
    for t in range(texts):
        logprobs[t] = combined[t] - lse[:, t:t + 1]
        column = jnp.where(at_pos == at_lane, score[:, t:t + 1], 0.0)
        target[t:t + 1, :] = jnp.sum(column, axis=0, keepdims=True)


def body(n, nv, private_logits, public_logits, noise, owner, counts, tokens):
    rows, pos, width = private_logits.shape
    texts, _, piece = public_logits.shape
    half = n // 2
    full = width // LANES
    win = max(-(-((j * piece) % LANES + piece) // LANES) for j in range(n))
    while min(j * piece - LANES * min(j * piece // LANES, full + 1 - win) for j in range(n)) < 0:
        win += 1
    win += win % 2
    wl = win * LANES
    hl = wl // 2
    bf16, f32, i16 = jnp.bfloat16, jnp.float32, jnp.int16
    smem = pl.BlockSpec(memory_space=pltpu.SMEM)
    vmem = pl.BlockSpec(memory_space=pltpu.VMEM)
    dma = pltpu.SemaphoreType.DMA
    combined, stats = pl.pallas_call(
        functools.partial(kernel, n, nv, rows, texts, pos, width, piece, win),
        out_shape=(
            jax.ShapeDtypeStruct((texts, pos, piece), f32),
            jax.ShapeDtypeStruct((2, pos, LANES), f32),
        ),
        in_specs=[smem, smem, smem, pl.BlockSpec(memory_space=pl.ANY), vmem, vmem],
        out_specs=(pl.BlockSpec(memory_space=pl.ANY), vmem),
        scratch_shapes=[
            pltpu.VMEM((texts, pos, piece), f32),
            pltpu.VMEM((rows, pos, width), bf16),
            pltpu.VMEM((rows, pos, n * LANES), bf16),
            pltpu.VMEM((texts, pos, wl), f32),
            pltpu.VMEM((n, texts, 2 * pos, hl), bf16),
            pltpu.VMEM((texts, 2 * pos, hl), f32),
            pltpu.VMEM((rows + 1, 2 * pos, hl), f32),
            pltpu.VMEM((half, texts, 2 * pos, hl), f32),
            pltpu.VMEM((half, texts, 2 * pos, hl), i16),
            pltpu.VMEM((half, texts, 2 * pos, hl), i16),
            pltpu.VMEM((half, texts, 2 * pos, hl), i16),
            pltpu.VMEM((half, texts, 2 * pos, hl), i16),
            pltpu.VMEM((n, 2 * pos, LANES), jnp.int32),
            pltpu.VMEM((nv, 2 * pos, LANES), f32),
            pltpu.VMEM((n, 2 * pos, LANES), f32),
            pltpu.VMEM((rows, 2 * pos, LANES), f32),
            pltpu.SMEM((rows,), jnp.int32),
            pltpu.SMEM((rows,), jnp.int32),
            pltpu.SMEM((texts + 1,), jnp.int32),
            dma, dma, dma,
            dma((half,)), dma((half,)), dma((half,)), dma((n,)),
            dma((half,)), dma((half,)), dma((half,)),
            dma((half,)), dma((half,)), dma((half,)), dma((half,)),
            dma, dma, dma, dma, dma,
        ],
        compiler_params=pltpu.CompilerParams(
            collective_id=0, has_side_effects=True, vmem_limit_bytes=56 * 1024 * 1024
        ),
        cost_estimate=pl.CostEstimate(
            flops=6 * rows * pos * width, bytes_accessed=2 * rows * pos * width, transcendentals=0
        ),
        name="private_scores",
    )(owner, counts, tokens, private_logits, public_logits, noise)
    return pl.pallas_call(
        functools.partial(finish, texts, pos),
        out_shape=(
            jax.ShapeDtypeStruct((texts, pos, piece), f32),
            jax.ShapeDtypeStruct((texts, pos), f32),
        ),
        in_specs=[vmem, vmem],
        out_specs=(vmem, vmem),
        name="subtract_lse",
    )(combined, stats)


def solution(mesh):
    return jax.shard_map(
        functools.partial(body, mesh.shape["ref"], mesh.shape["voc"]),
        mesh=mesh,
        in_specs=(
            P("ref", None, "voc"),
            P(None, None, ("voc", "ref")),
            P(None, None, ("voc", "ref")),
            P("ref"),
            P(),
            P(),
        ),
        out_specs=(P(None, None, ("voc", "ref")), P()),
        check_vma=False,
    )
```

```python
import functools

import jax
import jax.numpy as jnp
from jax import lax
from jax.experimental import pallas as pl
from jax.experimental.pallas import tpu as pltpu
from jax.sharding import PartitionSpec as P

clip_bound = 2.0
LANES = 128
MESH = pl.DeviceIdType.MESH


def fixed_point(rows):
    scale = 1
    while scale * 2 * clip_bound * rows <= 32000:
        scale *= 2
    return float(scale)


def turned(pairs):
    return (pairs + 3) // 6


def kernel(
    n, nv, rows, texts, pos, width, piece, win,
    owner, counts, tokens, priv, pub, noise,
    combined_hbm, stats_out,
    combined_out,    pv, xt, pubf, pubs, here, pref, keep, snd1, rs1, snd2, rs2, rowb, sndb, rsb, sndf, rsf,
    hist, st1, st2, bnd, order, sown, start,
    priv_sem, hist_s, hist_r, ag_x, ag_up, ag_dn, ag_r, agb_up, agb_dn, agb_r,
    rs1_s, rs1_r, rs2_s, rs2_r, rsb_s, rsb_r, rsf_s, rsf_r,
    st1_s, st1_r, st2_s, st2_r, out_sem,
):
    f32 = jnp.float32
    half = n // 2
    full = width // LANES
    wl = win * LANES
    pairs = win // 2
    hl = pairs * LANES
    hb = turned(pairs) * LANES
    me = lax.axis_index("ref")
    mv = lax.axis_index("voc")
    z = lax.div(me, 2)
    x = lax.rem(me, 2)
    partner = me + 1 - 2 * x
    scale1 = fixed_point(rows)
    scale2 = fixed_point(min(2 * rows, n * rows // texts))
    scale3 = fixed_point(min(half * rows, n * rows // texts))

    def first_tile(j):
        return jnp.minimum(lax.div(j * piece, LANES), full + 1 - win)

    def remote(src, dst, send, recv, peer):
        return pltpu.make_async_remote_copy(
            src_ref=src, dst_ref=dst, send_sem=send, recv_sem=recv,
            device_id=peer, device_id_type=MESH,
        )

    load = pltpu.make_async_copy(priv, pv, priv_sem)
    load.start()
    barrier = pltpu.get_barrier_semaphore()

    def greet(k, c):
        pl.semaphore_signal(barrier, inc=1, device_id={"ref": lax.rem(me + k, n)}, device_id_type=MESH)
        return c

    def greet_voc(k, c):
        pl.semaphore_signal(barrier, inc=1, device_id={"voc": lax.rem(mv + k, nv)}, device_id_type=MESH)
        return c

    lax.fori_loop(1, n, greet, 0)
    lax.fori_loop(1, nv, greet_voc, 0)

    shift = me * piece - first_tile(me) * LANES
    pubf[...] = jnp.zeros_like(pubf)
    for t in range(texts):
        pubf[t, :, :piece] = pub[t].astype(f32)
    for t in range(texts):
        moved = pltpu.roll(pubf[t], shift, 1)
        pubs[me, t] = jnp.concatenate([moved[:, :hl], moved[:, hl:]], axis=0).astype(jnp.bfloat16)

    own = [owner[r] for r in range(rows)]
    hits = [sum((o == t).astype(jnp.int32) for o in own) for t in range(texts)]
    lane8 = lax.broadcasted_iota(jnp.int32, (2 * pos, LANES), 1)
    mine = jnp.zeros((2 * pos, LANES), jnp.int32)
    for t in range(texts):
        mine = jnp.where(lane8 == t, hits[t], mine)
    hist[me] = mine

    pl.semaphore_wait(barrier, n - 1 + nv - 1)

    def whole(j):
        return pubs.at[j]

    def straight(j):
        return pubs.at[j, :, :, pl.ds(hb, hl - hb)]

    def turning(j):
        return pubs.at[j, :, :, pl.ds(0, hb)]

    def to_partner(part, j, zi):
        return remote(part(j), part(j), ag_x.at[zi], ag_r.at[j], {"ref": partner})

    def along(part, j, zi, up, down, recv):
        @pl.when((zi <= z) & (z < half - 1))
        def _():
            remote(part(j), part(j), up.at[zi], recv, {"ref": me + 2}).start()

        @pl.when((zi >= z) & (z > 0))
        def _():
            remote(part(j), part(j), down.at[zi], recv, {"ref": me - 2}).start()

    def pass_turned(zi):
        j = 2 * zi + 1 - x
        along(turning, j, zi, agb_up, agb_dn, agb_r.at[zi])

    def send_hist(k, c):
        remote(hist.at[me], hist.at[me], hist_s, hist_r, {"ref": lax.rem(me + k, n)}).start()
        return c

    lax.fori_loop(1, n, send_hist, 0)
    to_partner(whole, me, z).start()
    along(whole, me, z, ag_up, ag_dn, ag_r.at[me])

    begin = [jnp.int32(0)]
    for t in range(texts):
        begin.append(begin[-1] + hits[t])
    for t in range(texts + 1):
        start[t] = begin[t]
    place = []
    for r in range(rows):
        before = jnp.int32(0)
        for q in range(rows):
            if q < r:
                before = before + (own[q] <= own[r]).astype(jnp.int32)
            elif q > r:
                before = before + (own[q] < own[r]).astype(jnp.int32)
        place.append(before)
    for k in range(rows):
        at = jnp.int32(0)
        for r in range(rows):
            at = at + jnp.where(place[r] == k, r, 0)
        order[k] = at
        sown[k] = sum((begin[t] <= k).astype(jnp.int32) for t in range(1, texts))

    load.wait()
    for j in range(n):
        s = min(j * piece // LANES, full + 1 - win) + win - 1
        if s < full:
            xt[:, :, j * LANES:(j + 1) * LANES] = pv[:, :, s * LANES:(s + 1) * LANES]
        else:
            xt[:, :, j * LANES:(j + 1) * LANES] = jnp.zeros((rows, pos, LANES), jnp.bfloat16)
            if width > full * LANES:
                xt[:, :, j * LANES:j * LANES + width - full * LANES] = pv[:, :, full * LANES:]

    got = hist.at[pl.ds(0, n - 1)]
    pltpu.make_async_copy(got, got, hist_r).wait()
    pltpu.make_async_copy(got, got, hist_s).wait()
    lower = jnp.zeros((2 * pos, LANES), jnp.int32)
    lower = lax.fori_loop(0, n, lambda j, a: a + jnp.where(j < me, hist[j], 0), lower)
    lane4 = lane8[:pos]
    pref[0] = jnp.zeros_like(pref[0])
    for k in range(rows):
        text = sown[k]
        limit = counts[text] - (k - start[text])
        ok = jnp.where((lane8 == text) & (lower < limit), clip_bound, 0.0)
        bnd[k] = jnp.broadcast_to(jnp.max(ok, axis=1, keepdims=True), (2 * pos, LANES))

    def partial_sums(j, store):
        base = first_tile(j) * LANES
        for t in range(texts):
            here[t] = pubs[j, t].astype(f32)
        base = pl.multiple_of(base, LANES)
        middle = pl.multiple_of(base + hl, LANES)
        end = pl.multiple_of(j * LANES, LANES)
        acc = jnp.zeros((2 * pos, hl), f32)
        for k in range(rows):
            row = order[k]
            b = jnp.concatenate([bnd[k]] * pairs, axis=1)
            low = pv[row, :, pl.ds(base, hl)].astype(f32)
            high = pv[row, :, pl.ds(middle, hl - LANES)].astype(f32)
            high = jnp.concatenate([high, xt[row, :, pl.ds(end, LANES)].astype(f32)], axis=1)
            p = jnp.concatenate([low, high], axis=0)
            acc = acc + jnp.minimum(jnp.maximum(p - here[sown[k]], -b), b)
            pref[k + 1] = acc
        for t in range(texts):
            store(t, pref[start[t + 1]] - pref[start[t]])

    def coded(v, scale):
        return jnp.round(v * scale).astype(jnp.int32).astype(jnp.int16)

    def decoded(q, scale):
        return q.astype(jnp.int32).astype(f32) * (1.0 / scale)

    nearer = jnp.minimum(z, half - 1 - z)

    def column(i):
        side = jnp.where(lax.rem(i, 2) == 1, -lax.div(i + 1, 2), lax.div(i, 2))
        rest = jnp.where(z < half - 1 - z, i, half - 1 - i)
        return jnp.where(i <= 2 * nearer, z + side, rest)

    def own_column(i):
        zi = column(i)

        def store(t, v):
            keep[zi, t] = v

        partial_sums(2 * zi + x, store)

    def take_turned(i):
        zi = column(i)
        part = turning(2 * zi + 1 - x)
        remote(part, part, agb_up.at[zi], agb_r.at[zi], {"ref": partner}).wait_recv()
        pass_turned(zi)

    def other_column(i, c):
        zi = column(lax.rem(i, half))
        j = 2 * zi + 1 - x

        @pl.when(i < half)
        def _():
            to_partner(straight, j, zi).wait_recv()

        def store(t, v):
            snd1[zi, t] = coded(v[:, hb:], scale1)
            sndb[zi, t] = coded(v[:, :hb], scale1)
            rowb[t] = v[:, :hb]

        partial_sums(j, store)
        remote(snd1.at[zi], rs1.at[zi], rs1_s.at[zi], rs1_r.at[zi], {"ref": partner}).start()

        @pl.when(i < half)
        def _():
            remote(sndb.at[zi], rsb.at[z], rsb_s.at[zi], rsb_r.at[z], {"ref": 2 * zi + x}).start()

        return c

    def arrive(i, c):
        zi = column(i)
        j = 2 * zi + x
        to_partner(whole, j, zi).wait_recv()
        to_partner(straight, j, zi).start()
        along(whole, j, zi, ag_up, ag_dn, ag_r.at[j])

        @pl.when(i >= 2)
        def _():
            take_turned(i - 1)
            other_column(i - 1, 0)

        return c

    def add_partner(i, c):
        zi = column(lax.rem(i, half))

        @pl.when(i < half)
        def _():
            own_column(i)

        remote(snd1.at[zi], rs1.at[zi], rs1_s.at[zi], rs1_r.at[zi], {"ref": partner}).wait_recv()
        for t in range(texts):
            keep[zi, t, :, hb:] = keep[zi, t, :, hb:] + decoded(rs1[zi, t], scale1)

        @pl.when(i < half)
        def _():
            for t in range(texts):
                snd2[zi, t] = coded(keep[zi, t], scale2)
            remote(snd2.at[zi], rs2.at[z], rs2_s.at[zi], rs2_r.at[z], {"ref": 2 * zi + x}).start()

        return c

    def add_turned(k, c):
        zi = lax.rem(z + k, half)
        remote(sndb.at[zi], rsb.at[zi], rsb_s.at[zi], rsb_r.at[zi], {"ref": 2 * zi + x}).wait_recv()
        for t in range(texts):
            rowb[t] = rowb[t] + decoded(rsb[zi, t], scale1)
        return c

    def gather(k, c):
        zi = lax.rem(z + k, half)
        remote(snd2.at[zi], rs2.at[zi], rs2_s.at[zi], rs2_r.at[zi], {"ref": 2 * zi + x}).wait_recv()
        for t in range(texts):
            keep[z, t] = keep[z, t] + decoded(rs2[zi, t], scale2)
        return c

    own_column(jnp.int32(0))
    to_partner(whole, 2 * z + 1 - x, z).wait_recv()
    pass_turned(z)
    lax.fori_loop(1, half, arrive, 0)
    take_turned(jnp.int32(half - 1))
    lax.fori_loop(half - 1, half + 1, other_column, 0)
    lax.fori_loop(1, half + 1, add_partner, 0)
    lax.fori_loop(1, half, add_turned, 0)
    for t in range(texts):
        sndf[t] = coded(rowb[t], scale3)
    last = remote(sndf, rsf, rsf_s, rsf_r, {"ref": partner})
    last.start()
    lax.fori_loop(1, half, gather, 0)
    last.wait_recv()
    for t in range(texts):
        keep[z, t, :, :hb] = keep[z, t, :, :hb] + decoded(rsf[t], scale3)

    first_column = (mv * n + me) * piece
    at_column = lax.broadcasted_iota(jnp.int32, (pos, piece), 1) + first_column
    at_pos = lax.broadcasted_iota(jnp.int32, (pos, 1), 0)
    lse_all = jnp.zeros((pos, LANES), f32)
    picked_all = jnp.zeros((pos, LANES), f32)
    for t in range(texts):
        both = keep[z, t]
        summed = jnp.concatenate([both[:pos], both[pos:]], axis=1)
        summed = pltpu.roll(summed, lax.rem(wl - shift, wl), 1)[:, :piece]
        root = jnp.sqrt(jnp.full((pos, LANES), counts[t].astype(f32), f32))
        factor = (1.0 / (clip_bound * root))[:, :1]
        combined = pub[t].astype(f32) + summed * factor + noise[t].astype(f32)
        combined_out[t] = combined
        peak = jnp.max(combined, axis=1, keepdims=True)
        total = jnp.sum(jnp.exp(combined - peak), axis=1, keepdims=True)
        token = jnp.zeros((pos, 1), jnp.int32)
        for p in range(pos):
            token = jnp.where(at_pos == p, tokens[t, p], token)
        picked = jnp.sum(jnp.where(at_column == token, combined, 0.0), axis=1, keepdims=True)
        lse_all = jnp.where(lane4 == t, peak + jnp.log(total), lse_all)
        picked_all = jnp.where(lane4 == t, picked, picked_all)

    out = pltpu.make_async_copy(combined_out, combined_hbm, out_sem)
    out.start()

    def exchange(slots, send, recv, index, count, axis, lse, picked):
        slots[index, :pos] = lse
        slots[index, pos:2 * pos] = picked

        def send_one(k, c):
            remote(slots.at[index], slots.at[index], send, recv, {axis: lax.rem(index + k, count)}).start()
            return c

        lax.fori_loop(1, count, send_one, 0)
        others = slots.at[pl.ds(0, count - 1)]
        pltpu.make_async_copy(others, others, recv).wait()
        top = lax.fori_loop(1, count, lambda j, a: jnp.maximum(a, slots[j, :pos]), slots[0, :pos])
        zero = jnp.zeros((pos, LANES), f32)
        total, found = lax.fori_loop(
            0, count,
            lambda j, a: (a[0] + jnp.exp(slots[j, :pos] - top), a[1] + slots[j, pos:2 * pos]),
            (zero, zero),
        )
        return top + jnp.log(total), found

    lse, picked = exchange(st1, st1_s, st1_r, mv, nv, "voc", lse_all, picked_all)
    lse, picked = exchange(st2, st2_s, st2_r, me, n, "ref", lse, picked)
    stats_out[0] = lse
    stats_out[1] = picked
    out.wait()

    for slots, count, send in ((st1, nv, st1_s), (st2, n, st2_s)):
        others = slots.at[pl.ds(0, count - 1)]
        pltpu.make_async_copy(others, others, send).wait()

    def left(src, sem):
        remote(src, src, sem, ag_r.at[me], {"ref": partner}).wait_send()

    def sent(i, c):
        left(snd1.at[i], rs1_s.at[i])

        @pl.when((i <= z) & (z < half - 1))
        def _():
            left(whole(me), ag_up.at[i])
            left(turning(me), agb_up.at[i])

        @pl.when((i >= z) & (z > 0))
        def _():
            left(whole(me), ag_dn.at[i])
            left(turning(me), agb_dn.at[i])

        @pl.when(i != z)
        def _():
            left(straight(me), ag_x.at[i])
            left(snd2.at[i], rs2_s.at[i])
            left(sndb.at[i], rsb_s.at[i])

        return c

    left(whole(me), ag_x.at[z])
    left(sndf, rsf_s)
    lax.fori_loop(0, half, sent, 0)


def finish(texts, pos, combined, stats, logprobs, target):
    lse = stats[0]
    score = stats[1] - lse
    at_pos = lax.broadcasted_iota(jnp.int32, (pos, pos), 0)
    at_lane = lax.broadcasted_iota(jnp.int32, (pos, pos), 1)
    for t in range(texts):
        logprobs[t] = combined[t] - lse[:, t:t + 1]
        column = jnp.where(at_pos == at_lane, score[:, t:t + 1], 0.0)
        target[t:t + 1, :] = jnp.sum(column, axis=0, keepdims=True)


def body(n, nv, private_logits, public_logits, noise, owner, counts, tokens):
    rows, pos, width = private_logits.shape
    texts, _, piece = public_logits.shape
    half = n // 2
    full = width // LANES
    win = max(-(-((j * piece) % LANES + piece) // LANES) for j in range(n))
    while min(j * piece - LANES * min(j * piece // LANES, full + 1 - win) for j in range(n)) < 0:
        win += 1
    win += win % 2
    wl = win * LANES
    hl = wl // 2
    hb = turned(win // 2) * LANES
    bf16, f32, i16 = jnp.bfloat16, jnp.float32, jnp.int16
    smem = pl.BlockSpec(memory_space=pltpu.SMEM)
    vmem = pl.BlockSpec(memory_space=pltpu.VMEM)
    dma = pltpu.SemaphoreType.DMA
    combined, stats = pl.pallas_call(
        functools.partial(kernel, n, nv, rows, texts, pos, width, piece, win),
        out_shape=(
            jax.ShapeDtypeStruct((texts, pos, piece), f32),
            jax.ShapeDtypeStruct((2, pos, LANES), f32),
        ),
        in_specs=[smem, smem, smem, pl.BlockSpec(memory_space=pl.ANY), vmem, vmem],
        out_specs=(pl.BlockSpec(memory_space=pl.ANY), vmem),
        scratch_shapes=[
            pltpu.VMEM((texts, pos, piece), f32),
            pltpu.VMEM((rows, pos, width), bf16),
            pltpu.VMEM((rows, pos, n * LANES), bf16),
            pltpu.VMEM((texts, pos, wl), f32),
            pltpu.VMEM((n, texts, 2 * pos, hl), bf16),
            pltpu.VMEM((texts, 2 * pos, hl), f32),
            pltpu.VMEM((rows + 1, 2 * pos, hl), f32),
            pltpu.VMEM((half, texts, 2 * pos, hl), f32),
            pltpu.VMEM((half, texts, 2 * pos, hl - hb), i16),
            pltpu.VMEM((half, texts, 2 * pos, hl - hb), i16),
            pltpu.VMEM((half, texts, 2 * pos, hl), i16),
            pltpu.VMEM((half, texts, 2 * pos, hl), i16),
            pltpu.VMEM((texts, 2 * pos, hb), f32),
            pltpu.VMEM((half, texts, 2 * pos, hb), i16),
            pltpu.VMEM((half, texts, 2 * pos, hb), i16),
            pltpu.VMEM((texts, 2 * pos, hb), i16),
            pltpu.VMEM((texts, 2 * pos, hb), i16),
            pltpu.VMEM((n, 2 * pos, LANES), jnp.int32),
            pltpu.VMEM((nv, 2 * pos, LANES), f32),
            pltpu.VMEM((n, 2 * pos, LANES), f32),
            pltpu.VMEM((rows, 2 * pos, LANES), f32),
            pltpu.SMEM((rows,), jnp.int32),
            pltpu.SMEM((rows,), jnp.int32),
            pltpu.SMEM((texts + 1,), jnp.int32),
            dma, dma, dma,
            dma((half,)), dma((half,)), dma((half,)), dma((n,)),
            dma((half,)), dma((half,)), dma((half,)),
            dma((half,)), dma((half,)), dma((half,)), dma((half,)),
            dma((half,)), dma((half,)), dma, dma,
            dma, dma, dma, dma, dma,
        ],
        compiler_params=pltpu.CompilerParams(
            collective_id=0, has_side_effects=True, vmem_limit_bytes=56 * 1024 * 1024
        ),
        cost_estimate=pl.CostEstimate(
            flops=6 * rows * pos * width, bytes_accessed=2 * rows * pos * width, transcendentals=0
        ),
        name="private_scores",
    )(owner, counts, tokens, private_logits, public_logits, noise)
    return pl.pallas_call(
        functools.partial(finish, texts, pos),
        out_shape=(
            jax.ShapeDtypeStruct((texts, pos, piece), f32),
            jax.ShapeDtypeStruct((texts, pos), f32),
        ),
        in_specs=[vmem, vmem],
        out_specs=(vmem, vmem),
        name="subtract_lse",
    )(combined, stats)


def solution(mesh):
    return jax.shard_map(
        functools.partial(body, mesh.shape["ref"], mesh.shape["voc"]),
        mesh=mesh,
        in_specs=(
            P("ref", None, "voc"),
            P(None, None, ("voc", "ref")),
            P(None, None, ("voc", "ref")),
            P("ref"),
            P(),
            P(),
        ),
        out_specs=(P(None, None, ("voc", "ref")), P()),
        check_vma=False,
    )
```
